256 devices in a mesh: front: 16 (over x, z_lo, core), row: 4 (over z_hi), col: 4 (over y).
Axes of the slice: x: 4, y: 4, z: 8 (z_hi: 4, z_lo: 2; z = z_hi * 2 + z_lo), core: 2. Of those that a mesh axis runs over, the one named last changes fastest.
Arguments:
- front_entries: float32 [65536, 4096], P(('front', 'row'), 'col'), parts along dimension 0, may hold values from -2 to 8, as said below
- child_updates: bfloat16 [65536, 2048], P(('front', 'row'), 'col'), parts along dimension 0, may hold values from -1 to 1, as said below
- child_maps: int32 [32, 16], P('front'), parts along dimension 0, may hold values from 0 to 31, as said below
Outputs:
- factored: float32 [65536, 4096], P(('front', 'row'), 'col'), parts along dimension 0
The draws below stay inside these ranges and needn't reach their ends.
There are 16 independent parts, one for each index of `front`. The reference program is written for one: setup_inputs(seed, part) draws one part's arguments, and reference() takes and returns one part's arrays. A program takes and returns all parts, laid end to end along the dimension named above; each array names one. Nothing has to cross between parts.
Inputs may be any that keep to these rules, and one draw needn't show every extreme that they name: `front_entries`: symmetric; every diagonal entry of the rows from 1024 on lies in 3.5 to 7; the leading 1024 x 1024 block of the assembled front is positive definite. `child_updates`: each sibling's 2048 x 2048 block is symmetric. `child_maps`: each row lists 2048/128 distinct parent block numbers in decreasing order and contains every block number below 8.
All inputs are finite; a program needn't handle non-finite values.
Results may differ from the reference program's by a relative error of at most 0.0003.
Values may be sent and summed in bfloat16 or wider, within the bound.
A program may use at most 128 MiB of HBM per device.

```python
import jax
import jax.numpy as jnp
from jax import lax

F = 4096
P_SIZE = 1024
CU = 2048
NB = 128


def parent_blocks(key):
    total = F // NB
    pivots = P_SIZE // NB
    taken = CU // NB - pivots
    others = total - pivots
    spare = jax.random.permutation(jax.random.fold_in(key, 11), others - 1).astype(jnp.int32) + pivots
    second = jax.random.permutation(jax.random.fold_in(key, 12), others).astype(jnp.int32) + pivots
    heading = jnp.arange(pivots, dtype=jnp.int32)
    last_block = jnp.full((1,), total - 1, jnp.int32)
    first_sibling = jnp.concatenate([heading, last_block, spare[:taken - 1]])
    second_sibling = jnp.concatenate([heading, second[:taken]])
    ordered = jnp.stack([jnp.sort(first_sibling), jnp.sort(second_sibling)])
    return jnp.flip(ordered, axis=1).astype(jnp.int32)


def stiffness_links(key, extent, spread):
    positions = jnp.arange(extent, dtype=jnp.int32)
    distance = jnp.abs(positions[:, None] - positions[None, :])
    levels = distance // spread
    powers = jnp.array([2 ** (10 - exponent) for exponent in range(11)], jnp.int32)
    strength = powers[jnp.minimum(levels, 10)]
    drawn = jax.random.randint(key, (extent, extent), 0, 8, jnp.int32)
    paired = drawn + drawn.T
    linked = jnp.where((levels <= 10) & (distance > 0), paired * strength, 0).astype(jnp.int32)
    degree = jnp.sum(linked, axis=1).astype(jnp.int32)
    same = positions[:, None] == positions[None, :]
    return (linked, degree, same)


def draw_child_maps(key, part):
    return parent_blocks(key)


def draw_child_updates(key, part):
    blocks = parent_blocks(key)
    key = jax.random.fold_in(key, 3)
    pivot_rows = (jnp.repeat(blocks, NB, axis=1) < P_SIZE // NB).astype(jnp.float32)
    spread = max(P_SIZE // 64, 1)
    scaling_base = 2.0 ** (-(16 + spread.bit_length() - 1))
    updates = []
    for sibling in range(2):
        subkey = jax.random.fold_in(key, sibling)
        sampled = jnp.clip(0.5 * jax.random.normal(subkey, (CU, CU), jnp.float32), -1.0, 1.0)
        symmetric = 0.5 * (sampled + sampled.T)
        linked, degree, same = stiffness_links(jax.random.fold_in(subkey, 9), P_SIZE, spread)
        stiffness = jnp.where(same, degree[:, None], -linked).astype(jnp.float32) * scaling_base
        padded = jnp.pad(stiffness, ((CU - P_SIZE, 0), (CU - P_SIZE, 0)))
        marker = pivot_rows[sibling]
        inside_both = marker[:, None] * marker[None, :]
        inside_one = marker[:, None] + marker[None, :] - 2.0 * inside_both
        outside = 1.0 - inside_both - inside_one
        scaling = inside_one * 0.2 + outside * 0.8
        updates.append(jnp.where(inside_both > 0.5, padded, symmetric * scaling))
    return jnp.concatenate(updates, axis=0).astype(jnp.bfloat16)


def draw_front_entries(key, part):
    key = jax.random.fold_in(key, 5)
    positions = jnp.arange(F, dtype=jnp.int32)
    pivot_mark = (positions < P_SIZE).astype(jnp.float32)
    inside_both = pivot_mark[:, None] * pivot_mark[None, :]
    inside_one = pivot_mark[:, None] + pivot_mark[None, :] - 2.0 * inside_both
    outside = 1.0 - inside_both - inside_one
    spread = max(P_SIZE // 64, 1)
    exponent_base = 13 + spread.bit_length() - 1
    scaling_base = 2.0 ** (-exponent_base)
    lowest = -(-2 ** exponent_base // 100)
    linked, degree, same = stiffness_links(jax.random.fold_in(key, 7), P_SIZE, spread)
    doubling_table = jnp.array([1, 2, 4, 8], jnp.int32)
    doubling = doubling_table[jax.random.randint(jax.random.fold_in(key, 8), (P_SIZE,), 0, 4, jnp.int32)]
    extra = jax.random.randint(jax.random.fold_in(key, 9), (P_SIZE,), 0, lowest, jnp.int32)
    shifted = degree + lowest * doubling + extra
    stiffness = jnp.where(same, shifted[:, None], -linked).astype(jnp.float32) * scaling_base
    padded = jnp.pad(stiffness, ((0, F - P_SIZE), (0, F - P_SIZE)))
    sampled = jnp.clip(jax.random.normal(jax.random.fold_in(key, 2), (F, F), jnp.float32), -3.0, 3.0) / 3.0
    symmetric = 0.5 * (sampled + sampled.T)
    coupling = 1.2 * symmetric
    diagonal = 3.5 + 3.5 * jax.random.uniform(jax.random.fold_in(key, 3), (F,), jnp.float32)
    off_diagonal = inside_one * coupling + outside * symmetric
    rest = jnp.where(positions[:, None] == positions[None, :], diagonal[:, None], off_diagonal)
    return jnp.where(inside_both > 0.5, padded, rest)


def setup_inputs(seed: int = 0, part: int = 0) -> dict:
    streams_of = jax.random.split(jax.random.key(seed), 4)
    part_keys = jax.random.split(jax.random.fold_in(streams_of[3], part), 4)
    front_entries = draw_front_entries(jax.random.fold_in(jax.random.fold_in(streams_of[3], part), 71), part)
    child_updates = draw_child_updates(jax.random.fold_in(jax.random.fold_in(streams_of[3], part), 71), part)
    child_maps = draw_child_maps(jax.random.fold_in(jax.random.fold_in(streams_of[3], part), 71), part)
    return dict(front_entries=front_entries, child_updates=child_updates, child_maps=child_maps)


def expand_blocks(block_map):
    within = jnp.arange(NB, dtype=jnp.int32)
    return (block_map[:, None].astype(jnp.int32) * NB + within[None, :]).reshape(-1)

def reference(front_entries, child_updates, child_maps):
    assembled = front_entries.astype(jnp.float32)
    for sibling in range(2):
        targets = expand_blocks(child_maps[sibling])
        update = child_updates[sibling * CU:(sibling + 1) * CU].astype(jnp.float32)
        assembled = assembled.at[targets[:, None], targets[None, :]].add(update)
    pivot_factor = jnp.linalg.cholesky(assembled[:P_SIZE, :P_SIZE])
    below_rows = jax.scipy.linalg.solve_triangular(pivot_factor, assembled[P_SIZE:, :P_SIZE].T, lower=True).T
    schur_block = assembled[P_SIZE:, P_SIZE:] - jnp.dot(below_rows.astype(jnp.float32), below_rows.T.astype(jnp.float32), precision=lax.Precision.HIGHEST, preferred_element_type=jnp.float32)
    upper_rows = jnp.concatenate([pivot_factor, jnp.zeros((P_SIZE, F - P_SIZE), jnp.float32)], axis=1)
    lower_rows = jnp.concatenate([below_rows, schur_block], axis=1)
    return jnp.concatenate([upper_rows, lower_rows], axis=0)
```

```python
import functools

import jax
import jax.numpy as jnp
from jax import lax
from jax.experimental import pallas as pl
from jax.experimental.pallas import tpu as pltpu
from jax.sharding import PartitionSpec as P

MESH = pl.DeviceIdType.MESH
HIGHEST = lax.Precision.HIGHEST
T = 1024
NB = 128
QR = 256
STEPS = T // NB
G = 8
HALF = T // 2

R_PIV = 0
R_FWD = 16
R_BWD = 18
R_CROSS = 20
R_PART = 23
R_CH0, R_CH0B, R_CH1 = 27, 28, 29
R_YL, R_YR, R_Y2 = 30, 32, 34
R_PAN = 36
R_PANY = 44
N_RECV = 76

S_PIV = 0
S_FB = 8
S_CROSS = 12
S_PART = 14
S_CH = 16
S_REL = 18
S_Y = 20
S_Y2 = 24
S_ROOT = 26
S_PANZ = 66
S_PANY = 82
N_SEND = 106


def dot_t(a, b):
    return lax.dot_general(
        a, b, (((1,), (1,)), ((), ())), precision=HIGHEST, preferred_element_type=jnp.float32
    )


def split3(x):
    high = x.astype(jnp.bfloat16).astype(jnp.float32)
    rest = x - high
    middle = rest.astype(jnp.bfloat16).astype(jnp.float32)
    return high, middle, rest - middle


def eliminate_rows(g, work, upper, inverse):
    first = pl.multiple_of(g * G, G)
    rows = work[pl.ds(first, G), :]
    block, carried = rows[:, :NB], rows[:, NB:]
    turned = pltpu.roll(block, lax.rem(NB - first, NB), 1)
    sub = lax.broadcasted_iota(jnp.int32, (G, NB), 0)
    lane = lax.broadcasted_iota(jnp.int32, (G, NB), 1)
    columns = [jnp.broadcast_to(turned[:, j : j + 1], (G, NB)) for j in range(G)]
    scale = jnp.ones((G, NB), jnp.float32)
    for j in range(G):
        pivot = jnp.broadcast_to(columns[j][j : j + 1, :], (G, NB))
        scale = jnp.where(sub == j, pivot, scale)
        if j == G - 1:
            break
        factor = jnp.where(sub > j, columns[j] / pivot, 0.0)
        for i in range(j + 1, G):
            columns[i] = columns[i] - factor * columns[i][j : j + 1, :]
        block = block - factor * block[j : j + 1, :]
        carried = carried - factor * carried[j : j + 1, :]
    root = lax.rsqrt(scale)
    root = root * (1.5 - 0.5 * scale * root * root)
    block = jnp.where(lane >= first + sub, block * root, 0.0)
    carried = carried * root
    upper[pl.ds(first, G), :] = block
    inverse[pl.ds(first, G), :] = carried
    both = jnp.concatenate([block, carried], axis=1)
    high, middle, low = split3(both)
    left = jnp.concatenate(
        [high[:, :NB], high[:, :NB], middle[:, :NB], middle[:, :NB], high[:, :NB], low[:, :NB]], axis=0
    )
    right = jnp.concatenate([high, middle, high, middle, low, high], axis=0)
    work[...] -= jnp.dot(
        left.T.astype(jnp.bfloat16), right.astype(jnp.bfloat16), preferred_element_type=jnp.float32
    )


def spread_kernel(front, child, ar, ac, ch, bz, lp, tile, low, panels, pivots, work, upper, inverse, ssem, rsem, lsem):
    f, r, c = lax.axis_index("front"), lax.axis_index("row"), lax.axis_index("col")
    root = (r == 0) & (c == 0)
    lower = r >= 1
    odd = lax.rem(r, 2) == 1
    right, left = lax.rem(c + 1, 4), lax.rem(c + 3, 4)
    others = [1 + lax.rem(jnp.maximum(r, 1) - 1 + d, 3) for d in (1, 2)]
    piv_source = odd & (c >= 2)
    pending = []

    barrier = pltpu.get_barrier_semaphore()

    def greet(row, col):
        pl.semaphore_signal(barrier, inc=1, device_id=(f, row, col), device_id_type=MESH)

    for d in (1, 2, 3):
        greet(r, lax.rem(c + d, 4))
        greet(lax.rem(r + d, 4), c)

    @pl.when(root)
    def _():
        for row in (1, 3):
            for col in (2, 3):
                greet(row, col)
        pl.semaphore_wait(barrier, 10)

    @pl.when(piv_source)
    def _():
        greet(0, 0)
        pl.semaphore_wait(barrier, 7)

    @pl.when(jnp.logical_not(root | piv_source))
    def _():
        pl.semaphore_wait(barrier, 6)

    def remote(src, dst, sid, rid, row, col):
        return pltpu.make_async_remote_copy(
            src_ref=src, dst_ref=dst, send_sem=ssem.at[sid], recv_sem=rsem.at[rid],
            device_id=(f, row, col), device_id_type=MESH,
        )

    def send(cond, make):
        @pl.when(cond)
        def _():
            make().start()

        pending.append((cond, lambda: make().wait_send()))

    def arrived(ref, rid):
        remote(ref, ref, 0, rid, lax.rem(r + 1, 4), c).wait_recv()

    def quarter(ref, q):
        return ref.at[pl.ds(q * QR, QR)]

    for k in range(STEPS):
        h, t = divmod(STEPS - 1 - k, 4)
        part = (pl.ds(0, T - k * NB), pl.ds(t * NB, NB))
        send(
            odd & (c == 2 + h),
            lambda h=h, k=k, part=part: remote(
                child.at[part], pivots.at[(lax.div(r, 2), h) + part], S_PIV + k,
                R_PIV + lax.div(r, 2) * 8 + k, 0, 0,
            ),
        )

    for n, row in enumerate((1, 3)):
        for source, slot, rid in ((0, 0, R_CH0), (2, 1, R_CH1)):
            send(
                r == source,
                lambda row=row, slot=slot, rid=rid, n=n: remote(child, ch.at[slot, c], S_CH + n, rid, row, c),
            )
    keep_child = lambda: pltpu.make_async_copy(child, ch.at[1, c], lsem.at[0])

    @pl.when(r == 2)
    def _():
        keep_child().start()

    start_rows = lower & (c == 0)
    for i, (ahead, behind) in enumerate(((1, 3), (2, 0))):
        send(start_rows, lambda q=ahead, i=i: remote(quarter(front, q), quarter(ar, q), S_FB + i, R_FWD + i, r, 1))
        send(start_rows, lambda q=behind, i=i: remote(quarter(front, q), quarter(ar, q), S_FB + 2 + i, R_BWD + i, r, 3))

    def cross(cond, src):
        for n, row in enumerate(others):
            send(cond, lambda n=n, row=row: remote(src(), bz.at[r - 1], S_CROSS + n, R_CROSS + r - 1, row, c))

    cross(start_rows, lambda: quarter(front, 0))
    keep_front = lambda: pltpu.make_async_copy(front, ar, lsem.at[1])

    @pl.when(start_rows)
    def _():
        keep_front().start()

    relays = lower & (c >= 1)
    for i, (ahead, behind) in enumerate(((1, 3), (2, 0))):
        @pl.when(relays)
        def _(i=i, q=ahead):
            arrived(quarter(ar, q), R_FWD + i)

        send(relays & (c < 3), lambda q=ahead, i=i: remote(quarter(ar, q), quarter(ar, q), S_FB + i, R_FWD + i, r, c + 1))
        cross(lower & (c == ahead), lambda q=ahead: quarter(ar, q))

        @pl.when(relays)
        def _(i=i, q=behind):
            arrived(quarter(ar, q), R_BWD + i)

        send(relays & (c > 1), lambda q=behind, i=i: remote(quarter(ar, q), quarter(ar, q), S_FB + 2 + i, R_BWD + i, r, c - 1))
        if behind:
            cross(lower & (c == behind), lambda q=behind: quarter(ar, q))

    upper_half, lower_half = pl.ds(0, HALF), pl.ds(HALF, HALF)

    @pl.when(odd)
    def _():
        arrived(ch.at[0, c], R_CH0)

    send(r == 1, lambda: remote(ch.at[0, c, upper_half], ch.at[0, c, upper_half], S_REL, R_CH0, 2, c))
    send(r == 3, lambda: remote(ch.at[0, c, lower_half], ch.at[0, c, lower_half], S_REL, R_CH0B, 2, c))

    @pl.when(odd)
    def _():
        arrived(ch.at[1, c], R_CH1)

    @pl.when(r == 2)
    def _():
        arrived(ch.at[0, c, upper_half], R_CH0)
        arrived(ch.at[0, c, lower_half], R_CH0B)
        keep_child().wait()

    for s in range(2):
        send(lower, lambda s=s: remote(ch.at[s, c], ch.at[s, c], S_Y + s, R_YL + s, r, right))
        send(lower, lambda s=s: remote(ch.at[s, c], ch.at[s, c], S_Y + 2 + s, R_YR + s, r, left))

    for n, row in enumerate(others):
        @pl.when(lower)
        def _(row=row):
            arrived(bz.at[row - 1], R_CROSS + row - 1)

        send(
            lower & (c != row),
            lambda n=n, row=row: remote(bz.at[row - 1], quarter(ac, c), S_PART + n, R_PART + c, r, row),
        )

        @pl.when(lower & (c == row))
        def _(row=row):
            pltpu.make_async_copy(bz.at[row - 1], quarter(ac, c), lsem.at[2]).start()

    @pl.when(lower)
    def _():
        arrived(ch.at[0, left], R_YL)

    send(lower, lambda: remote(ch.at[0, left], ch.at[0, left], S_Y2, R_Y2, r, right))

    @pl.when(lower)
    def _():
        arrived(ch.at[1, right], R_YR + 1)

    send(lower, lambda: remote(ch.at[1, right], ch.at[1, right], S_Y2 + 1, R_Y2 + 1, r, left))

    def share(ref, k, q):
        return ref.at[k, pl.ds(q * 32, 32), pl.ds(0, NB * (k + 1))]

    def root_sends(k):
        made = []
        for q in (1, 3, 2):
            made.append(remote(share(panels, k, q), share(lp, k, q), S_ROOT + 5 * k + q, R_PAN + k, 0, q))
        for n, row in enumerate((1, 3)):
            made.append(remote(share(panels, k, 0), share(lp, k, 0), S_ROOT + 5 * k + 3 * n * 4 // 3, R_PAN + k, row, 0))
        return made

    @pl.when(root)
    def _():
        load = pltpu.make_async_copy(front, tile, lsem.at[0])
        load.start()
        low[...] = jnp.zeros_like(low)
        load.wait()
        ones = (
            lax.broadcasted_iota(jnp.int32, (NB, NB), 0) == lax.broadcasted_iota(jnp.int32, (NB, NB), 1)
        ).astype(jnp.float32)
        for k in range(STEPS):
            h, t = divmod(STEPS - 1 - k, 4)
            done, here = pl.ds(0, k * NB), pl.ds(k * NB, NB)
            for s in range(2):
                arrived(pivots.at[s, h, pl.ds(0, T - k * NB), pl.ds(t * NB, NB)], R_PIV + s * 8 + k)

            def updated(i, h=h, t=t, k=k, done=done, here=here):
                rows = pl.ds(pl.multiple_of(i * NB, NB), NB)
                source = pl.ds(pl.multiple_of((STEPS - 1 - i) * NB, NB), NB)
                value = tile[rows, here]
                for s in range(2):
                    value = value + pivots[s, h, source, pl.ds(t * NB, NB)].astype(jnp.float32)
                if k:
                    value = value - dot_t(low[rows, done], low[here, done])
                return value

            work[:, :NB] = updated(k)
            work[:, NB:] = ones

            def group(g, carry):
                eliminate_rows(g, work, upper, inverse)
                return carry

            lax.fori_loop(0, NB // G, group, 0)
            low[here, here] = upper[...].T
            if k:
                panels[k, :, pl.ds(0, k * NB)] = low[here, done]
            panels[k, :, pl.ds(k * NB, NB)] = inverse[...]
            for copy in root_sends(k):
                copy.start()

            def below(i, carry, updated=updated, here=here):
                low[pl.ds(pl.multiple_of(i * NB, NB), NB), here] = dot_t(updated(i), inverse[...])
                return carry

            if k + 1 < STEPS:
                lax.fori_loop(k + 1, STEPS, below, 0)
        store = pltpu.make_async_copy(low, ar, lsem.at[0])
        store.start()
        store.wait()
        for k in range(STEPS):
            for copy in root_sends(k):
                copy.wait_send()

    for k in range(STEPS):
        @pl.when(jnp.logical_not(root))
        def _(k=k):
            arrived(share(lp, k, c), R_PAN + k)

        for n, row in enumerate((1, 3)):
            send(
                (r == 0) & (c >= 1),
                lambda k=k, n=n, row=row: remote(share(lp, k, c), share(lp, k, c), S_PANZ + 2 * k + n, R_PAN + k, row, c),
            )
        send(
            r == (1 if k % 2 == 0 else 3),
            lambda k=k: remote(share(lp, k, c), share(lp, k, c), S_PANZ + 2 * k, R_PAN + k, 2, c),
        )
        for d in (1, 3, 2):
            send(
                lower,
                lambda k=k, d=d: remote(
                    share(lp, k, c), share(lp, k, c), S_PANY + 3 * k + d - 1, R_PANY + 4 * k + c, r, lax.rem(c + d, 4)
                ),
            )

    @pl.when(lower)
    def _():
        arrived(ch.at[0, right], R_YR)
        arrived(ch.at[1, left], R_YL + 1)
        arrived(ch.at[0, lax.rem(c + 2, 4)], R_Y2)
        arrived(ch.at[1, lax.rem(c + 2, 4)], R_Y2 + 1)

    @pl.when(start_rows)
    def _():
        keep_front().wait()

    @pl.when(lower & (c >= 1) & (c != r))
    def _():
        pltpu.make_async_copy(bz.at[c - 1], quarter(ac, c), lsem.at[2]).wait()
        for d in (1, 2, 3):
            q = lax.rem(c + d, 4)
            arrived(quarter(ac, q), R_PART + q)

    @pl.when(lower)
    def _():
        for k in range(STEPS):
            for d in (1, 2, 3):
                q = lax.rem(c + d, 4)
                arrived(share(lp, k, q), R_PANY + 4 * k + q)

    for cond, wait in pending:
        pl.when(cond)(wait)


def spread(front, child):
    shape = jax.ShapeDtypeStruct
    anywhere = pl.BlockSpec(memory_space=pl.ANY)
    return pl.pallas_call(
        spread_kernel,
        out_shape=[
            shape((T, T), jnp.float32),
            shape((T, T), jnp.float32),
            shape((2, 4, T, HALF), jnp.bfloat16),
            shape((3, QR, T), jnp.float32),
            shape((STEPS, NB, T), jnp.float32),
        ],
        in_specs=[anywhere] * 2,
        out_specs=[anywhere] * 5,
        scratch_shapes=[
            pltpu.VMEM((T, T), jnp.float32),
            pltpu.VMEM((T, T), jnp.float32),
            pltpu.VMEM((STEPS, NB, T), jnp.float32),
            pltpu.VMEM((2, 2, T, HALF), jnp.bfloat16),
            pltpu.VMEM((NB, 2 * NB), jnp.float32),
            pltpu.VMEM((NB, NB), jnp.float32),
            pltpu.VMEM((NB, NB), jnp.float32),
            pltpu.SemaphoreType.DMA((N_SEND,)),
            pltpu.SemaphoreType.DMA((N_RECV,)),
            pltpu.SemaphoreType.DMA((3,)),
        ],
        compiler_params=pltpu.CompilerParams(
            collective_id=0, has_side_effects=True, vmem_limit_bytes=40 * 2**20
        ),
    )(front, child)


def split2(x):
    high = x.astype(jnp.bfloat16)
    return high, (x - high.astype(jnp.float32)).astype(jnp.bfloat16)


def dot3(ah, al, bh, bl):
    dims = (((1,), (1,)), ((), ()))
    one = lambda a, b: lax.dot_general(a, b, dims, preferred_element_type=jnp.float32)
    return one(ah, bh) + (one(ah, bl) + one(al, bh))


def finish_kernel(places, front, ar, ac, ch, lp, out, a, kids, pan, acc, xh, xl, panh, panl, sems, osem):
    r, c = lax.axis_index("row"), lax.axis_index("col")
    schur = (r >= 1) & (c >= 1)
    lone = (c == 0) | (c == r)
    blocks = jnp.where(lone, STEPS, 2 * STEPS)

    @pl.when((r == 0) & (c == 0))
    def _():
        copy = pltpu.make_async_copy(ar, out, osem.at[0])
        copy.start()
        copy.wait()

    @pl.when((r == 0) & (c > 0))
    def _():
        acc[...] = jnp.zeros_like(acc)
        copy = pltpu.make_async_copy(acc, out, osem.at[0])
        copy.start()
        copy.wait()

    @pl.when(r >= 1)
    def _():
        load_a = pltpu.make_async_copy(ar, a.at[pl.ds(0, T)], sems.at[0])
        load_b = pltpu.make_async_copy(ac, a.at[pl.ds(T, T)], sems.at[1])
        load_np = pltpu.make_async_copy(ch.at[:, pl.ds(2, 2)], kids.at[:, pl.ds(2, 2)], sems.at[2])
        load_nn = pltpu.make_async_copy(ch.at[:, pl.ds(0, 2)], kids.at[:, pl.ds(0, 2)], sems.at[3])
        load_front = pltpu.make_async_copy(front, acc, sems.at[4])
        load_pan = [
            pltpu.make_async_copy(
                lp.at[k, :, pl.ds(0, NB * (k + 1))], pan.at[k, :, pl.ds(0, NB * (k + 1))], sems.at[5 + k]
            )
            for k in range(STEPS)
        ]
        load_a.start()
        load_np.start()
        pl.when(jnp.logical_not(lone))(load_b.start)
        for copy in load_pan:
            copy.start()
        load_front.start()
        load_nn.start()
        load_a.wait()
        load_np.wait()
        pl.when(jnp.logical_not(lone))(load_b.wait)

        def assemble(b, carry):
            parent = jnp.where(b < STEPS, STEPS * r + b, STEPS * c + b - STEPS)
            rows = pl.ds(pl.multiple_of(b * NB, NB), NB)
            for s in range(2):
                j = places[s, parent]

                @pl.when(j >= 0)
                def _(s=s, j=j):
                    source = pl.ds(pl.multiple_of(j * NB, NB), NB)
                    for h in range(2):
                        for t in range(4):
                            columns = pl.ds((STEPS - 1 - 4 * h - t) * NB, NB)
                            a[rows, columns] += kids[s, 2 + h, source, pl.ds(t * NB, NB)].astype(jnp.float32)
            return carry

        lax.fori_loop(0, blocks, assemble, 0)

        for k in range(STEPS):
            load_pan[k].wait()
            done, here = pl.ds(0, k * NB), pl.ds(k * NB, NB)
            panh[:, pl.ds(0, NB * (k + 1))], panl[:, pl.ds(0, NB * (k + 1))] = split2(pan[k, :, pl.ds(0, NB * (k + 1))])

            def solve(i, carry, k=k, done=done, here=here):
                rows = pl.ds(pl.multiple_of(i * QR, QR), QR)
                value = a[rows, here]
                if k:
                    value = value - dot3(xh[rows, done], xl[rows, done], panh[:, done], panl[:, done])
                vh, vl = split2(value)
                solved = dot3(vh, vl, panh[:, here], panl[:, here])
                a[rows, here] = solved
                xh[rows, here], xl[rows, here] = split2(solved)
                return carry

            lax.fori_loop(0, lax.div(blocks, 2), solve, 0)

        load_front.wait()
        load_nn.wait()

        @pl.when(c == 0)
        def _():
            copy = pltpu.make_async_copy(a.at[pl.ds(0, T)], out, osem.at[0])
            copy.start()
            copy.wait()

    @pl.when(schur)
    def _():
        def add_rows(b, carry):
            rows = pl.ds(pl.multiple_of(b * NB, NB), NB)
            for s in range(2):
                j = places[s, STEPS * r + b]

                @pl.when(j >= 0)
                def _(s=s, j=j):
                    source = pl.ds(pl.multiple_of(j * NB, NB), NB)
                    for d in range(STEPS):
                        i = places[s, STEPS * c + d]

                        @pl.when(i >= 0)
                        def _(s=s, d=d, i=i):
                            from_columns = pl.ds(pl.multiple_of(lax.rem(i, 4) * NB, NB), NB)
                            acc[rows, pl.ds(d * NB, NB)] += kids[s, lax.div(i, 4), source, from_columns].astype(
                                jnp.float32
                            )
            return carry

        lax.fori_loop(0, STEPS, add_rows, 0)
        second = jnp.where(lone, 0, T)

        def push(i):
            rows = pl.ds(pl.multiple_of(i * QR, QR), QR)
            return pltpu.make_async_copy(acc.at[rows], out.at[rows], osem.at[i])

        def product(i, carry):
            rows = pl.ds(pl.multiple_of(i * QR, QR), QR)
            for j in range(4):
                others = pl.ds(pl.multiple_of(second + j * QR, QR), QR)
                columns = pl.ds(j * QR, QR)
                acc[rows, columns] -= dot3(xh[rows, :], xl[rows, :], xh[others, :], xl[others, :])
            push(i).start()
            return carry

        lax.fori_loop(0, 4, product, 0)
        for i in range(4):
            push(i).wait()


def finish(places, front, ar, ac, ch, lp):
    anywhere = pl.BlockSpec(memory_space=pl.ANY)
    return pl.pallas_call(
        finish_kernel,
        out_shape=jax.ShapeDtypeStruct((T, T), jnp.float32),
        in_specs=[pl.BlockSpec(memory_space=pltpu.SMEM)] + [anywhere] * 5,
        out_specs=anywhere,
        scratch_shapes=[
            pltpu.VMEM((2 * T, T), jnp.float32),
            pltpu.VMEM((2, 4, T, HALF), jnp.bfloat16),
            pltpu.VMEM((STEPS, NB, T), jnp.float32),
            pltpu.VMEM((T, T), jnp.float32),
            pltpu.VMEM((2 * T, T), jnp.bfloat16),
            pltpu.VMEM((2 * T, T), jnp.bfloat16),
            pltpu.VMEM((NB, T), jnp.bfloat16),
            pltpu.VMEM((NB, T), jnp.bfloat16),
            pltpu.SemaphoreType.DMA((13,)),
            pltpu.SemaphoreType.DMA((4,)),
        ],
        compiler_params=pltpu.CompilerParams(vmem_limit_bytes=52 * 2**20),
    )(places, front, ar, ac, ch, lp)


def local(front_entries, child_updates, child_maps):
    found = child_maps[:, :, None] == jnp.arange(4 * STEPS, dtype=jnp.int32)[None, None, :]
    order = jnp.arange(1, child_maps.shape[1] + 1, dtype=jnp.int32)
    places = jnp.sum(jnp.where(found, order[None, :, None], 0), axis=1) - 1
    ar, ac, ch, _, lp = spread(front_entries, child_updates)
    return finish(places, front_entries, ar, ac, ch, lp)


def solution(mesh):
    placed = (P(("front", "row"), "col"), P(("front", "row"), "col"), P("front", None))
    return jax.shard_map(
        local, mesh=mesh, in_specs=placed, out_specs=P(("front", "row"), "col"), check_vma=False
    )
```

```python
import functools

import jax
import jax.numpy as jnp
from jax import lax
from jax.experimental import pallas as pl
from jax.experimental.pallas import tpu as pltpu
from jax.sharding import PartitionSpec as P

MESH = pl.DeviceIdType.MESH
HIGHEST = lax.Precision.HIGHEST
T = 1024
NB = 128
QR = 256
STEPS = T // NB
G = 8
HALF = T // 2

R_PIV = 0
R_FRONT = 16
R_NP = 17
R_NN = 19
R_ROWS = 21
R_CROSS = 25
R_PART = 28
R_NNY = 32
R_PAN = 40
R_PANY = 48
N_RECV = 80

S_PIV = 0
S_FRONT = 8
S_CHILD = 11
S_ROWS = 17
S_CROSS = 20
S_PART = 22
S_NNY = 24
S_ROOT = 30
S_PANZ = 78
S_PANY = 102
N_SEND = 126


def dot_t(a, b):
    return lax.dot_general(
        a, b, (((1,), (1,)), ((), ())), precision=HIGHEST, preferred_element_type=jnp.float32
    )


def split3(x):
    high = x.astype(jnp.bfloat16).astype(jnp.float32)
    rest = x - high
    middle = rest.astype(jnp.bfloat16).astype(jnp.float32)
    return high, middle, rest - middle


def eliminate_rows(g, work, upper, inverse):
    first = pl.multiple_of(g * G, G)
    rows = work[pl.ds(first, G), :]
    block, carried = rows[:, :NB], rows[:, NB:]
    turned = pltpu.roll(block, lax.rem(NB - first, NB), 1)
    sub = lax.broadcasted_iota(jnp.int32, (G, NB), 0)
    lane = lax.broadcasted_iota(jnp.int32, (G, NB), 1)
    columns = [jnp.broadcast_to(turned[:, j : j + 1], (G, NB)) for j in range(G)]
    scale = jnp.ones((G, NB), jnp.float32)
    for j in range(G):
        pivot = jnp.broadcast_to(columns[j][j : j + 1, :], (G, NB))
        scale = jnp.where(sub == j, pivot, scale)
        if j == G - 1:
            break
        factor = jnp.where(sub > j, columns[j] / pivot, 0.0)
        for i in range(j + 1, G):
            columns[i] = columns[i] - factor * columns[i][j : j + 1, :]
        block = block - factor * block[j : j + 1, :]
        carried = carried - factor * carried[j : j + 1, :]
    root = lax.rsqrt(scale)
    root = root * (1.5 - 0.5 * scale * root * root)
    block = jnp.where(lane >= first + sub, block * root, 0.0)
    carried = carried * root
    upper[pl.ds(first, G), :] = block
    inverse[pl.ds(first, G), :] = carried
    both = jnp.concatenate([block, carried], axis=1)
    high, middle, low = split3(both)
    left = jnp.concatenate(
        [high[:, :NB], high[:, :NB], middle[:, :NB], middle[:, :NB], high[:, :NB], low[:, :NB]], axis=0
    )
    right = jnp.concatenate([high, middle, high, middle, low, high], axis=0)
    work[...] -= jnp.dot(
        left.T.astype(jnp.bfloat16), right.astype(jnp.bfloat16), preferred_element_type=jnp.float32
    )


def spread_kernel(
    picks, front, child, ar, ac, nn, bz, lp, fq, npq, tile, low, panels, pivots, work, upper, inverse, ssem, rsem, lsem
):
    f, r, c = lax.axis_index("front"), lax.axis_index("row"), lax.axis_index("col")
    root = (r == 0) & (c == 0)
    lower = r >= 1
    odd = lax.rem(r, 2) == 1
    others = [1 + lax.rem(jnp.maximum(r, 1) - 1 + d, 3) for d in (1, 2)]
    around = [lax.rem(c + d, 4) for d in (1, 3, 2)]
    piv_source = odd & (c >= 2)
    child_source = (r == 0) | (r == 2)
    pending = []

    barrier = pltpu.get_barrier_semaphore()
    for row in range(4):
        for d in range(4):
            col = lax.rem(c + d, 4)

            @pl.when((row != r) | (d != 0))
            def _(row=row, col=col):
                pl.semaphore_signal(barrier, inc=1, device_id=(f, row, col), device_id_type=MESH)

    pl.semaphore_wait(barrier, 15)

    def remote(src, dst, sid, rid, row, col):
        return pltpu.make_async_remote_copy(
            src_ref=src, dst_ref=dst, send_sem=ssem.at[sid], recv_sem=rsem.at[rid],
            device_id=(f, row, col), device_id_type=MESH,
        )

    def send(cond, make):
        @pl.when(cond)
        def _():
            make().start()

        pending.append((cond, lambda: make().wait_send()))

    def arrived(ref, rid):
        remote(ref, ref, 0, rid, lax.rem(r + 1, 4), c).wait_recv()

    def quarter(ref, q):
        return ref.at[:, pl.ds(pl.multiple_of(q * QR, QR), QR)]

    for q in (2, 1, 3):
        send(lower & (c == 0), lambda q=q: remote(quarter(front, q), fq, S_FRONT + q - 1, R_FRONT, r, q))
    own_front = lambda: pltpu.make_async_copy(quarter(front, 0), fq, lsem.at[0])
    own_child = lambda: pltpu.make_async_copy(quarter(child, 1), npq.at[1], lsem.at[1])

    @pl.when(lower & (c == 0))
    def _():
        own_front().start()

    @pl.when((r == 2) & (c == 2))
    def _():
        own_child().start()

    sibling = lax.div(r, 2)
    for row in (2, 1, 3):
        for u in range(2):
            q_np = jnp.where(c < 2, 0, 7 - 2 * c - u)
            q_nn = jnp.where(c < 2, 2 * c + u, 0)
            sid = S_CHILD + 2 * (row - 1) + u
            send(
                child_source & (c >= 2) & ((r != row) | (q_np != c)),
                lambda u=u, q=q_np, row=row, sid=sid: remote(quarter(child, u), npq.at[sibling], sid, R_NP + sibling, row, q),
            )
            send(
                child_source & (c < 2) & ((r != row) | (q_nn != c)),
                lambda u=u, q=q_nn, row=row, sid=sid: remote(
                    quarter(child, u), quarter(nn.at[sibling], q), sid, R_NN + sibling, row, q
                ),
            )

    for k in range(STEPS):
        h, t = divmod(STEPS - 1 - k, 4)
        part = (pl.ds(0, T - k * NB), pl.ds(t * NB, NB))

        @pl.when(odd & (c == 2 + h))
        def _(h=h, k=k, part=part):
            copy = remote(
                child.at[part], pivots.at[(lax.div(r, 2), h) + part], S_PIV + k, R_PIV + lax.div(r, 2) * 8 + k, 0, 0
            )
            copy.start()
            copy.wait_send()

    @pl.when(lower & (c == 0))
    def _():
        own_front().wait()

    @pl.when(lower & (c != 0))
    def _():
        arrived(fq, R_FRONT)

    @pl.when((r == 2) & (c == 2))
    def _():
        own_child().wait()

    @pl.when(lower)
    def _():
        arrived(npq.at[0], R_NP)

    @pl.when(lower & ((r != 2) | (c != 2)))
    def _():
        arrived(npq.at[1], R_NP + 1)

    @pl.when(lower)
    def _():
        def assemble(b, carry):
            rows = pl.ds(pl.multiple_of(b * NB, NB), NB)
            for t in range(2):
                value = fq[rows, pl.ds(t * NB, NB)]
                for s in range(2):
                    for j in range(STEPS):
                        picked = picks[4 * STEPS * s + STEPS * r + b, j]
                        value += picked * npq[s, pl.ds(j * NB, NB), pl.ds((1 - t) * NB, NB)].astype(jnp.float32)
                fq[rows, pl.ds(t * NB, NB)] = value
            return carry

        lax.fori_loop(0, STEPS, assemble, 0)

    keep_rows = lambda: pltpu.make_async_copy(fq, quarter(ar, c), lsem.at[0])

    @pl.when(lower)
    def _():
        keep_rows().start()

    for n, row in enumerate(others):
        send(lower, lambda n=n, row=row: remote(fq, bz.at[r - 1], S_CROSS + n, R_CROSS + r - 1, row, c))
    for n, col in enumerate(around):
        send(lower, lambda n=n, col=col: remote(fq, quarter(ar, c), S_ROWS + n, R_ROWS + c, r, col))

    kept = (r == 2) & (c == 0)
    for s in range(2):
        came = lower & jnp.logical_not(kept) if s else lower

        @pl.when(came)
        def _(s=s):
            arrived(quarter(nn.at[s], c), R_NN + s)

        for n, col in enumerate(around):
            for cond, src in ((came, lambda s=s: quarter(nn.at[s], c)), (kept, lambda: quarter(child, 0))):
                if s or cond is came:
                    send(
                        cond & (col != 0),
                        lambda s=s, n=n, col=col, src=src: remote(
                            src(), quarter(nn.at[s], c), S_NNY + 3 * s + n, R_NNY + 4 * s + c, r, col
                        ),
                    )

    for n, row in enumerate(others):
        @pl.when(lower)
        def _(row=row):
            arrived(bz.at[row - 1], R_CROSS + row - 1)

        send(
            lower & (c != row),
            lambda n=n, row=row: remote(bz.at[row - 1], quarter(ac, c), S_PART + n, R_PART + c, r, row),
        )

    def share(ref, k, q):
        return ref.at[k, pl.ds(q * 32, 32), pl.ds(0, NB * (k + 1))]

    def root_sends(k):
        made = []
        for q in (1, 3, 2):
            made.append(remote(share(panels, k, q), share(lp, k, q), S_ROOT + 6 * k + q - 1, R_PAN + k, 0, q))
        for row in (1, 3, 2):
            made.append(remote(share(panels, k, 0), share(lp, k, 0), S_ROOT + 6 * k + 2 + row, R_PAN + k, row, 0))
        return made

    @pl.when(root)
    def _():
        load = pltpu.make_async_copy(front, tile, lsem.at[0])
        load.start()
        low[...] = jnp.zeros_like(low)
        load.wait()
        ones = (
            lax.broadcasted_iota(jnp.int32, (NB, NB), 0) == lax.broadcasted_iota(jnp.int32, (NB, NB), 1)
        ).astype(jnp.float32)
        for k in range(STEPS):
            h, t = divmod(STEPS - 1 - k, 4)
            done, here = pl.ds(0, k * NB), pl.ds(k * NB, NB)
            for s in range(2):
                arrived(pivots.at[s, h, pl.ds(0, T - k * NB), pl.ds(t * NB, NB)], R_PIV + s * 8 + k)

            def updated(i, h=h, t=t, k=k, done=done, here=here):
                rows = pl.ds(pl.multiple_of(i * NB, NB), NB)
                source = pl.ds(pl.multiple_of((STEPS - 1 - i) * NB, NB), NB)
                value = tile[rows, here]
                for s in range(2):
                    value = value + pivots[s, h, source, pl.ds(t * NB, NB)].astype(jnp.float32)
                if k:
                    value = value - dot_t(low[rows, done], low[here, done])
                return value

            work[:, :NB] = updated(k)
            work[:, NB:] = ones

            def group(g, carry):
                eliminate_rows(g, work, upper, inverse)
                return carry

            lax.fori_loop(0, NB // G, group, 0)
            low[here, here] = upper[...].T
            if k:
                panels[k, :, pl.ds(0, k * NB)] = low[here, done]
            panels[k, :, pl.ds(k * NB, NB)] = inverse[...]
            for copy in root_sends(k):
                copy.start()

            def below(i, carry, updated=updated, here=here):
                low[pl.ds(pl.multiple_of(i * NB, NB), NB), here] = dot_t(updated(i), inverse[...])
                return carry

            if k + 1 < STEPS:
                lax.fori_loop(k + 1, STEPS, below, 0)
        store = pltpu.make_async_copy(low, ar, lsem.at[0])
        store.start()
        store.wait()
        for k in range(STEPS):
            for copy in root_sends(k):
                copy.wait_send()

    for k in range(STEPS):
        @pl.when(jnp.logical_not(root))
        def _(k=k):
            arrived(share(lp, k, c), R_PAN + k)

        for n, row in enumerate((1, 3, 2)):
            send(
                (r == 0) & (c >= 1),
                lambda k=k, n=n, row=row: remote(share(lp, k, c), share(lp, k, c), S_PANZ + 3 * k + n, R_PAN + k, row, c),
            )
        for n, col in enumerate(around):
            send(
                lower,
                lambda k=k, n=n, col=col: remote(
                    share(lp, k, c), share(lp, k, c), S_PANY + 3 * k + n, R_PANY + 4 * k + c, r, col
                ),
            )

    @pl.when(lower)
    def _():
        keep_rows().wait()
        for q in around:
            arrived(quarter(ar, q), R_ROWS + q)

    @pl.when(lower & (c >= 1))
    def _():
        for s in range(2):
            for q in around:
                arrived(quarter(nn.at[s], q), R_NNY + 4 * s + q)

    @pl.when(lower & (c >= 1) & (c != r))
    def _():
        for q in around:
            arrived(quarter(ac, q), R_PART + q)

    @pl.when(lower)
    def _():
        for k in range(STEPS):
            for q in around:
                arrived(share(lp, k, q), R_PANY + 4 * k + q)

    for cond, wait in pending:
        pl.when(cond)(wait)


def spread(picks, front, child):
    shape = jax.ShapeDtypeStruct
    anywhere = pl.BlockSpec(memory_space=pl.ANY)
    return pl.pallas_call(
        spread_kernel,
        out_shape=[
            shape((T, T), jnp.float32),
            shape((T, T), jnp.float32),
            shape((2, T, T), jnp.bfloat16),
            shape((3, T, QR), jnp.float32),
            shape((STEPS, NB, T), jnp.float32),
        ],
        in_specs=[pl.BlockSpec(memory_space=pltpu.SMEM)] + [anywhere] * 2,
        out_specs=[anywhere] * 5,
        scratch_shapes=[
            pltpu.VMEM((T, QR), jnp.float32),
            pltpu.VMEM((2, T, QR), jnp.bfloat16),
            pltpu.VMEM((T, T), jnp.float32),
            pltpu.VMEM((T, T), jnp.float32),
            pltpu.VMEM((STEPS, NB, T), jnp.float32),
            pltpu.VMEM((2, 2, T, HALF), jnp.bfloat16),
            pltpu.VMEM((NB, 2 * NB), jnp.float32),
            pltpu.VMEM((NB, NB), jnp.float32),
            pltpu.VMEM((NB, NB), jnp.float32),
            pltpu.SemaphoreType.DMA((N_SEND,)),
            pltpu.SemaphoreType.DMA((N_RECV,)),
            pltpu.SemaphoreType.DMA((2,)),
        ],
        compiler_params=pltpu.CompilerParams(
            collective_id=0, has_side_effects=True, vmem_limit_bytes=40 * 2**20
        ),
    )(picks, front, child)


def split2(x):
    high = x.astype(jnp.bfloat16)
    return high, (x - high.astype(jnp.float32)).astype(jnp.bfloat16)


def dot3(ah, al, bh, bl):
    dims = (((1,), (1,)), ((), ()))
    one = lambda a, b: lax.dot_general(a, b, dims, preferred_element_type=jnp.float32)
    return one(ah, bh) + (one(ah, bl) + one(al, bh))


def finish_kernel(places, front, ar, ac, nn, bz, lp, out, a, kids, pan, acc, xh, xl, panh, panl, sems, osem):
    r, c = lax.axis_index("row"), lax.axis_index("col")
    schur = (r >= 1) & (c >= 1)
    lone = (c == 0) | (c == r)
    blocks = jnp.where(lone, STEPS, 2 * STEPS)

    @pl.when((r == 0) & (c == 0))
    def _():
        for source, target in ((ar, acc), (acc, out)):
            copy = pltpu.make_async_copy(source, target, osem.at[0])
            copy.start()
            copy.wait()

    @pl.when((r == 0) & (c > 0))
    def _():
        acc[...] = jnp.zeros_like(acc)
        copy = pltpu.make_async_copy(acc, out, osem.at[0])
        copy.start()
        copy.wait()

    @pl.when(r >= 1)
    def _():
        load_a = pltpu.make_async_copy(ar, a.at[pl.ds(0, T)], sems.at[0])
        load_b = []
        for q in range(4):
            columns = pl.ds(q * QR, QR)
            part, away = a.at[pl.ds(T, T), columns], jnp.logical_not(lone)
            load_b.append((away & (c != q), pltpu.make_async_copy(ac.at[:, columns], part, sems.at[1])))
            if q:
                load_b.append((away & (c == q), pltpu.make_async_copy(bz.at[q - 1], part, sems.at[1])))
        load_nn = pltpu.make_async_copy(nn, kids, sems.at[2])
        load_front = pltpu.make_async_copy(front, acc, sems.at[3])
        load_pan = [
            pltpu.make_async_copy(
                lp.at[k, :, pl.ds(0, NB * (k + 1))], pan.at[k, :, pl.ds(0, NB * (k + 1))], sems.at[4 + k]
            )
            for k in range(STEPS)
        ]
        load_a.start()
        for cond, copy in load_b:
            pl.when(cond)(copy.start)
        for copy in load_pan:
            copy.start()
        load_front.start()
        load_nn.start()
        load_a.wait()
        for cond, copy in load_b:
            pl.when(cond)(copy.wait)

        for k in range(STEPS):
            load_pan[k].wait()
            done, here = pl.ds(0, k * NB), pl.ds(k * NB, NB)
            panh[:, pl.ds(0, NB * (k + 1))], panl[:, pl.ds(0, NB * (k + 1))] = split2(pan[k, :, pl.ds(0, NB * (k + 1))])

            def solve(i, carry, k=k, done=done, here=here):
                rows = pl.ds(pl.multiple_of(i * QR, QR), QR)
                value = a[rows, here]
                if k:
                    value = value - dot3(xh[rows, done], xl[rows, done], panh[:, done], panl[:, done])
                vh, vl = split2(value)
                solved = dot3(vh, vl, panh[:, here], panl[:, here])
                a[rows, here] = solved
                xh[rows, here], xl[rows, here] = split2(solved)
                return carry

            lax.fori_loop(0, lax.div(blocks, 2), solve, 0)

        load_front.wait()
        load_nn.wait()

        @pl.when(c == 0)
        def _():
            copy = pltpu.make_async_copy(a.at[pl.ds(0, T)], out, osem.at[0])
            copy.start()
            copy.wait()

    @pl.when(schur)
    def _():
        def add_rows(b, carry):
            rows = pl.ds(pl.multiple_of(b * NB, NB), NB)
            for s in range(2):
                j = places[s, STEPS * r + b]

                @pl.when(j >= 0)
                def _(s=s, j=j):
                    source = pl.ds(pl.multiple_of(j * NB, NB), NB)
                    for d in range(STEPS):
                        i = places[s, STEPS * c + d]

                        @pl.when(i >= 0)
                        def _(s=s, d=d, i=i):
                            columns = pl.ds(pl.multiple_of(i * NB, NB), NB)
                            acc[rows, pl.ds(d * NB, NB)] += kids[s, source, columns].astype(jnp.float32)
            return carry

        lax.fori_loop(0, STEPS, add_rows, 0)
        second = jnp.where(lone, 0, T)

        def push(i):
            rows = pl.ds(pl.multiple_of(i * QR, QR), QR)
            return pltpu.make_async_copy(acc.at[rows], out.at[rows], osem.at[i])

        def product(i, carry):
            rows = pl.ds(pl.multiple_of(i * QR, QR), QR)
            for j in range(4):
                others = pl.ds(pl.multiple_of(second + j * QR, QR), QR)
                columns = pl.ds(j * QR, QR)
                acc[rows, columns] -= dot3(xh[rows, :], xl[rows, :], xh[others, :], xl[others, :])
            push(i).start()
            return carry

        lax.fori_loop(0, 4, product, 0)
        for i in range(4):
            push(i).wait()


def finish(places, front, ar, ac, nn, bz, lp):
    anywhere = pl.BlockSpec(memory_space=pl.ANY)
    return pl.pallas_call(
        finish_kernel,
        out_shape=jax.ShapeDtypeStruct((T, T), jnp.float32),
        in_specs=[pl.BlockSpec(memory_space=pltpu.SMEM)] + [anywhere] * 6,
        out_specs=anywhere,
        scratch_shapes=[
            pltpu.VMEM((2 * T, T), jnp.float32),
            pltpu.VMEM((2, T, T), jnp.bfloat16),
            pltpu.VMEM((STEPS, NB, T), jnp.float32),
            pltpu.VMEM((T, T), jnp.float32),
            pltpu.VMEM((2 * T, T), jnp.bfloat16),
            pltpu.VMEM((2 * T, T), jnp.bfloat16),
            pltpu.VMEM((NB, T), jnp.bfloat16),
            pltpu.VMEM((NB, T), jnp.bfloat16),
            pltpu.SemaphoreType.DMA((13,)),
            pltpu.SemaphoreType.DMA((4,)),
        ],
        compiler_params=pltpu.CompilerParams(vmem_limit_bytes=52 * 2**20),
    )(places, front, ar, ac, nn, bz, lp)


def local(front_entries, child_updates, child_maps):
    found = child_maps[:, :, None] == jnp.arange(4 * STEPS, dtype=jnp.int32)[None, None, :]
    order = jnp.arange(1, child_maps.shape[1] + 1, dtype=jnp.int32)
    places = jnp.sum(jnp.where(found, order[None, :, None], 0), axis=1) - 1
    picks = jnp.swapaxes(found[:, :STEPS], 1, 2).astype(jnp.float32).reshape(8 * STEPS, STEPS)
    return finish(places, front_entries, *spread(picks, front_entries, child_updates))


def solution(mesh):
    placed = (P(("front", "row"), "col"), P(("front", "row"), "col"), P("front", None))
    return jax.shard_map(
        local, mesh=mesh, in_specs=placed, out_specs=P(("front", "row"), "col"), check_vma=False
    )
```

```python
import functools

import jax
import jax.numpy as jnp
from jax import lax
from jax.experimental import pallas as pl
from jax.experimental.pallas import tpu as pltpu
from jax.sharding import PartitionSpec as P

MESH = pl.DeviceIdType.MESH
HIGHEST = lax.Precision.HIGHEST
T = 1024
NB = 128
QR = 256
STEPS = T // NB
G = 8
HALF = T // 2

R_PIV = 0
R_FRONT = 16
R_NPA = 17
R_NNA = 18
R_NP = 19
R_NN = 21
R_ROWS = 23
R_CROSS = 27
R_PART = 33
R_NNY = 41
R_PAN = 49
R_PANY = 57
R_HALF = 89
R_HELP = 90
N_RECV = 92

S_PIV = 0
S_FRONT = 8
S_AHEAD = 12
S_NP = 16
S_NN = 19
S_RELAY = 21
S_ROWS = 22
S_CROSS = 25
S_PART = 29
S_NNY = 33
S_HALF = 39
S_ROOT = 40
S_PANZ = 80
S_PANY = 96
N_SEND = 120


def dot_t(a, b):
    return lax.dot_general(
        a, b, (((1,), (1,)), ((), ())), precision=HIGHEST, preferred_element_type=jnp.float32
    )


def split3(x):
    high = x.astype(jnp.bfloat16).astype(jnp.float32)
    rest = x - high
    middle = rest.astype(jnp.bfloat16).astype(jnp.float32)
    return high, middle, rest - middle


def eliminate_rows(g, work, upper, inverse):
    first = pl.multiple_of(g * G, G)
    rows = work[pl.ds(first, G), :]
    block, carried = rows[:, :NB], rows[:, NB:]
    turned = pltpu.roll(block, lax.rem(NB - first, NB), 1)
    sub = lax.broadcasted_iota(jnp.int32, (G, NB), 0)
    lane = lax.broadcasted_iota(jnp.int32, (G, NB), 1)
    columns = [jnp.broadcast_to(turned[:, j : j + 1], (G, NB)) for j in range(G)]
    scale = jnp.ones((G, NB), jnp.float32)
    for j in range(G):
        pivot = jnp.broadcast_to(columns[j][j : j + 1, :], (G, NB))
        scale = jnp.where(sub == j, pivot, scale)
        if j == G - 1:
            break
        factor = jnp.where(sub > j, columns[j] / pivot, 0.0)
        for i in range(j + 1, G):
            columns[i] = columns[i] - factor * columns[i][j : j + 1, :]
        block = block - factor * block[j : j + 1, :]
        carried = carried - factor * carried[j : j + 1, :]
    root = lax.rsqrt(scale)
    root = root * (1.5 - 0.5 * scale * root * root)
    block = jnp.where(lane >= first + sub, block * root, 0.0)
    carried = carried * root
    upper[pl.ds(first, G), :] = block
    inverse[pl.ds(first, G), :] = carried
    both = jnp.concatenate([block, carried], axis=1)
    high, middle, low = split3(both)
    left = jnp.concatenate(
        [high[:, :NB], high[:, :NB], middle[:, :NB], middle[:, :NB], high[:, :NB], low[:, :NB]], axis=0
    )
    right = jnp.concatenate([high, middle, high, middle, low, high], axis=0)
    work[...] -= jnp.dot(
        left.T.astype(jnp.bfloat16), right.astype(jnp.bfloat16), preferred_element_type=jnp.float32
    )


def split2(x):
    high = x.astype(jnp.bfloat16)
    return high, (x - high.astype(jnp.float32)).astype(jnp.bfloat16)


def dot3(ah, al, bh, bl):
    dims = (((1,), (1,)), ((), ()))
    one = lambda a, b: lax.dot_general(a, b, dims, preferred_element_type=jnp.float32)
    return one(ah, bh) + (one(ah, bl) + one(al, bh))


def front_kernel(
    picks, front, child, out, nn, fq, npq, bz, a, lp, acc, xh, xl, panh, panl, work, upper, inverse, ssem, rsem, lsem
):
    f, r, c = lax.axis_index("front"), lax.axis_index("row"), lax.axis_index("col")
    root = (r == 0) & (c == 0)
    lower = r >= 1
    odd = lax.rem(r, 2) == 1
    others = [1 + lax.rem(jnp.maximum(r, 1) - 1 + d, 3) for d in (1, 2)]
    around = [lax.rem(c + d, 4) for d in (1, 3, 2)]
    piv_source = odd & (c >= 2)
    child_source = (r == 0) | (r == 2)
    pending = []

    barrier = pltpu.get_barrier_semaphore()
    for row in range(4):
        for d in range(4):
            col = lax.rem(c + d, 4)

            @pl.when((row != r) | (d != 0))
            def _(row=row, col=col):
                pl.semaphore_signal(barrier, inc=1, device_id=(f, row, col), device_id_type=MESH)

    pl.semaphore_wait(barrier, 15)

    def remote(src, dst, sid, rid, row, col):
        return pltpu.make_async_remote_copy(
            src_ref=src, dst_ref=dst, send_sem=ssem.at[sid], recv_sem=rsem.at[rid],
            device_id=(f, row, col), device_id_type=MESH,
        )

    def send(cond, make, waited=True):
        @pl.when(cond)
        def _():
            make().start()

        pending.append((cond if waited is True else waited, lambda: make().wait_send()))

    def arrived(ref, rid):
        remote(ref, ref, 0, rid, lax.rem(r + 1, 4), c).wait_recv()

    def quarter(ref, q):
        return ref.at[:, pl.ds(pl.multiple_of(q * QR, QR), QR)]

    def topped(ref, q, at=None):
        return ref.at[pl.ds(0, QR * (q + 1)), pl.ds((q if at is None else at) * QR, QR)]

    sibling = lax.div(r, 2)
    own_front = lambda: pltpu.make_async_copy(quarter(front, 0), fq, lsem.at[0])
    own_tile = lambda: pltpu.make_async_copy(front, acc, lsem.at[2])
    own_child = lambda: pltpu.make_async_copy(quarter(child, 1), npq.at[sibling], lsem.at[1])
    own_np = child_source & (c == 2)
    own_nn = child_source & (c == 0)

    @pl.when(lower & (c == 0))
    def _():
        own_front().start()

    @pl.when(own_np)
    def _():
        own_child().start()

    @pl.when(root | (lower & (c >= 1)))
    def _():
        own_tile().start()

    for u in range(2):
        q_np = jnp.where(c < 2, 0, 7 - 2 * c - u)
        send(
            child_source & (c >= 2) & (q_np != c),
            lambda u=u, q=q_np: remote(quarter(child, u), npq.at[sibling], S_AHEAD + u, R_NPA, r, q),
        )

    for q in range(1, 4):
        send(
            child_source & (c == q // 2),
            lambda q=q: remote(topped(child, q, q % 2), topped(nn.at[sibling], q), S_AHEAD + q % 2, R_NNA, r, q),
        )

    for n, row in enumerate((1, 3)):
        send(root, lambda n=n, row=row: remote(topped(child, 0, 0), topped(nn.at[0], 0), S_NN + n, R_NN, row, 0))

    halves = [pl.ds(h * HALF, HALF) for h in range(2)]

    def cross(cond, src):
        for h, rows in enumerate(halves):
            for n, row in enumerate(others):
                send(
                    cond,
                    lambda h=h, n=n, row=row, rows=rows: remote(
                        src().at[rows], bz.at[r - 1, rows], S_CROSS + 2 * h + n, R_CROSS + 3 * h + r - 1, row, c
                    ),
                )

    first = lower & (c == 0)

    for h, col in enumerate((1, 3)):
        send(
            first,
            lambda h=h, col=col: remote(
                quarter(front, 2).at[halves[h]], bz.at[r - 1, halves[h]], S_FRONT + 2 * (col // 2), R_HELP + h, r, col
            ),
        )
    for n, q in enumerate((1, 3)):
        send(first, lambda n=n, q=q: remote(quarter(front, q), fq, S_FRONT + 1 + 2 * n, R_FRONT, r, q))

    for h, col in enumerate((1, 3)):
        @pl.when(lower & (c == col))
        def _(h=h):
            arrived(bz.at[r - 1, halves[h]], R_HELP + h)

        send(
            lower & (c == col),
            lambda h=h: remote(bz.at[r - 1, halves[h]], fq.at[halves[h]], S_RELAY, R_FRONT if h == 0 else R_HELP, r, 2),
        )

    for k in range(STEPS):
        h, t = divmod(STEPS - 1 - k, 4)
        rows = pl.ds(0, T - k * NB)

        @pl.when(odd & (c == 2 + h))
        def _(t=t, k=k, rows=rows):
            copy = remote(
                child.at[rows, pl.ds(t * NB, NB)],
                xh.at[pl.ds(pl.multiple_of(sibling * T, T), T - k * NB), pl.ds((STEPS - 1 - k) * NB, NB)],
                S_PIV + k, R_PIV + sibling * 8 + k, 0, 0,
            )
            copy.start()
            copy.wait_send()

    @pl.when(own_np)
    def _():
        own_child().wait()

    first_c = (r == 0) & (c != 0)

    @pl.when(child_source & (c != 2))
    def _():
        arrived(npq.at[sibling], R_NPA)

    for n, row in enumerate((1, 3, 2)):
        send(
            (r == 0) if row == 2 else child_source,
            lambda n=n, row=row: remote(npq.at[sibling], npq.at[sibling], S_NP + n, R_NP + sibling, row, c),
        )

    def other_columns(rows):
        for q in range(4):
            if q:
                @pl.when(rows & (c == q))
                def _(q=q):
                    arrived(topped(nn.at[sibling], q), R_NNA)

            for n, row in enumerate((1, 3)):
                src = (lambda q=q: topped(nn.at[sibling], q)) if q else (lambda: topped(child, 0, 0))
                send(
                    rows & (c == q),
                    lambda n=n, row=row, q=q, src=src: remote(
                        src(), topped(nn.at[sibling], q), S_NN + n, R_NN + sibling, row, c
                    ),
                )

    @pl.when(lower & ((c == 1) | (c == 3)))
    def _():
        arrived(fq, R_FRONT)

    @pl.when(lower & (c == 2))
    def _():
        arrived(fq.at[halves[0]], R_FRONT)
        arrived(fq.at[halves[1]], R_HELP)

    @pl.when(lower)
    def _():
        arrived(npq.at[0], R_NP)

    @pl.when(odd)
    def _():
        arrived(npq.at[1], R_NP + 1)

    cross(first, lambda: quarter(front, 0))
    cross(lower & (c != 0), lambda: fq)

    def assemble(source, target, row, low, high):
        def block(b, carry):
            rows = pl.ds(pl.multiple_of(b * NB, NB), NB)
            for t in range(2):
                value = source[rows, pl.ds(t * NB, NB)]
                for s in range(2):
                    for j in range(STEPS):
                        picked = picks[4 * STEPS * s + STEPS * row + b, j]
                        value += picked * npq[s, pl.ds(j * NB, NB), pl.ds((1 - t) * NB, NB)].astype(jnp.float32)
                target[rows, pl.ds(t * NB, NB)] = value
            return carry

        lax.fori_loop(low, high, block, 0)

    def rows_part(q):
        return quarter(a.at[pl.ds(0, T)], q)

    def cols_part(q):
        return quarter(a.at[pl.ds(T, T)], q)

    @pl.when(first)
    def _():
        own_front().wait()

    @pl.when(lower)
    def _():
        assemble(fq, rows_part(c), r, 0, STEPS)

    share_rows = lambda n: remote(rows_part(c), rows_part(c), S_ROWS + n, R_ROWS + c, r, around[n])

    @pl.when(lower)
    def _():
        for n in range(3):
            share_rows(n).start()

    def share(ref, k, q):
        return ref.at[k, pl.ds(q * 32, 32), pl.ds(0, NB * (k + 1))]

    def pass_on(k):
        @pl.when(jnp.logical_not(root))
        def _():
            arrived(share(lp, k, c), R_PAN + k)

        for n, row in enumerate((1, 3)):
            send(
                first_c,
                lambda k=k, n=n, row=row: remote(share(lp, k, c), share(lp, k, c), S_PANZ + 2 * k + n, R_PAN + k, row, c),
            )
        send(
            r == 1 + 2 * (k % 2),
            lambda k=k: remote(share(lp, k, c), share(lp, k, c), S_PANZ + 2 * k, R_PAN + k, 2, c),
        )
        for n, col in enumerate(around):
            send(
                lower,
                lambda k=k, n=n, col=col: remote(
                    share(lp, k, c), share(lp, k, c), S_PANY + 3 * k + n, R_PANY + 4 * k + c, r, col
                ),
            )

    pass_on(0)
    pass_on(1)
    other_columns(first_c | (r == 2))

    for h, half in enumerate(halves):
        for n, row in enumerate(others):
            @pl.when(lower)
            def _(h=h, half=half, row=row):
                arrived(bz.at[row - 1, half], R_CROSS + 3 * h + row - 1)

            @pl.when(lower & (c != row))
            def _(h=h, row=row):
                assemble(bz.at[row - 1], bz.at[row - 1], row, 4 * h, 4 * h + 4)

            @pl.when(lower & (c == row))
            def _(h=h, row=row):
                assemble(bz.at[row - 1], cols_part(c), row, 4 * h, 4 * h + 4)

            send(
                lower & (c != row),
                lambda h=h, half=half, n=n, row=row: remote(
                    bz.at[row - 1, half], cols_part(c).at[half], S_PART + 2 * h + n, R_PART + 4 * h + c, r, row
                ),
            )
        pass_on(2 + 2 * h)
        pass_on(3 + 2 * h)

    def to_row(s, cond, q, src):
        for n, col in enumerate(around):
            send(
                cond & (c == q) & (col != 0),
                lambda n=n, col=col: remote(
                    src(), topped(nn.at[s], q), S_NNY + 3 * s + n, R_NNY + 4 * s + c, r, col
                ),
            )

    for q in range(4):
        size = QR * (q + 1) // 2
        columns = pl.ds(q * QR, QR)
        ends = [(pl.ds(0, size), columns), (pl.ds(size, size), columns)]
        to_row(1, r == 2, q, (lambda q=q: topped(nn.at[1], q)) if q else (lambda: topped(child, 0, 0)))

        @pl.when(odd & (c == q))
        def _(q=q):
            arrived(topped(nn.at[1], q), R_NN + 1)

        to_row(1, odd, q, lambda q=q: topped(nn.at[1], q))

        @pl.when(odd & (c == q))
        def _(q=q):
            arrived(topped(nn.at[0], q), R_NN)

        for row, end, rid in ((1, 0, R_NN), (3, 1, R_HALF)):
            send(
                (r == row) & (c == q),
                lambda end=end, rid=rid, ends=ends: remote(nn.at[(0,) + ends[end]], nn.at[(0,) + ends[end]], S_HALF, rid, 2, c),
            )

        @pl.when((r == 2) & (c == q))
        def _(ends=ends):
            arrived(nn.at[(0,) + ends[0]], R_NN)
            arrived(nn.at[(0,) + ends[1]], R_HALF)

        to_row(0, lower, q, lambda q=q: topped(nn.at[0], q))
    pass_on(6)
    pass_on(7)

    def root_sends(k):
        made = []
        for q in (1, 3, 2):
            made.append(remote(share(lp, k, q), share(lp, k, q), S_ROOT + 5 * k + q - 1, R_PAN + k, 0, q))
        for n, row in enumerate((1, 3)):
            made.append(remote(share(lp, k, 0), share(lp, k, 0), S_ROOT + 5 * k + 3 + n, R_PAN + k, row, 0))
        return made

    result = lambda ref: pltpu.make_async_copy(ref, out, lsem.at[3])

    @pl.when(root)
    def _():
        low = a.at[pl.ds(0, T)]
        low[...] = jnp.zeros((T, T), jnp.float32)
        own_tile().wait()
        ones = (
            lax.broadcasted_iota(jnp.int32, (NB, NB), 0) == lax.broadcasted_iota(jnp.int32, (NB, NB), 1)
        ).astype(jnp.float32)
        for k in range(STEPS):
            done, here, there = pl.ds(0, k * NB), pl.ds(k * NB, NB), pl.ds((STEPS - 1 - k) * NB, NB)
            for s in range(2):
                arrived(xh.at[pl.ds(s * T, T - k * NB), there], R_PIV + s * 8 + k)

            def updated(i, k=k, done=done, here=here, there=there):
                rows = pl.ds(pl.multiple_of(i * NB, NB), NB)
                value = acc[rows, here]
                for s in range(2):
                    source = pl.ds(pl.multiple_of(s * T + (STEPS - 1 - i) * NB, NB), NB)
                    value = value + xh[source, there].astype(jnp.float32)
                if k:
                    value = value - dot_t(low[rows, done], low[here, done])
                return value

            work[:, :NB] = updated(k)
            work[:, NB:] = ones

            def group(g, carry):
                eliminate_rows(g, work, upper, inverse)
                return carry

            lax.fori_loop(0, NB // G, group, 0)
            low[here, here] = upper[...].T
            if k:
                lp[k, :, done] = low[here, done]
            lp[k, :, here] = inverse[...]
            for copy in root_sends(k):
                copy.start()

            def below(i, carry, updated=updated, here=here):
                low[pl.ds(pl.multiple_of(i * NB, NB), NB), here] = dot_t(updated(i), inverse[...])
                return carry

            if k + 1 < STEPS:
                lax.fori_loop(k + 1, STEPS, below, 0)
        result(low).start()
        result(low).wait()
        for k in range(STEPS):
            for copy in root_sends(k):
                copy.wait_send()

    @pl.when(first_c)
    def _():
        acc[...] = jnp.zeros_like(acc)
        result(acc).start()
        result(acc).wait()

    lone = (c == 0) | (c == r)
    away = lower & jnp.logical_not(lone)

    def solve(k, base):
        done, here, all_here = pl.ds(0, k * NB), pl.ds(k * NB, NB), pl.ds(0, NB * (k + 1))
        panh[:, all_here], panl[:, all_here] = split2(lp[k, :, all_here])

        def chunk(i, carry):
            rows = pl.ds(pl.multiple_of(base + i * QR, QR), QR)
            value = a[rows, here]
            if k:
                value = value - dot3(xh[rows, done], xl[rows, done], panh[:, done], panl[:, done])
            vh, vl = split2(value)
            solved = dot3(vh, vl, panh[:, here], panl[:, here])
            a[rows, here] = solved
            xh[rows, here], xl[rows, here] = split2(solved)
            return carry

        lax.fori_loop(0, T // QR, chunk, 0)

    @pl.when(lower)
    def _():
        for n in range(3):
            share_rows(n).wait_send()
        for q in around:
            arrived(rows_part(q), R_ROWS + q)
        for k in range(STEPS):
            for q in around:
                arrived(share(lp, k, q), R_PANY + 4 * k + q)
            solve(k, 0)

    @pl.when(first)
    def _():
        result(a.at[pl.ds(0, T)]).start()

    @pl.when(away)
    def _():
        for h, half in enumerate(halves):
            for q in around:
                arrived(cols_part(q).at[half], R_PART + 4 * h + q)
        for k in range(STEPS):
            solve(k, T)

    schur = lower & (c >= 1)

    @pl.when(schur)
    def _():
        own_tile().wait()
        second = jnp.where(lone, 0, T)

        def product(i, carry):
            rows = pl.ds(pl.multiple_of(i * QR, QR), QR)
            for j in range(4):
                other = pl.ds(pl.multiple_of(second + j * QR, QR), QR)
                columns = pl.ds(j * QR, QR)
                acc[rows, columns] -= dot3(xh[rows, :], xl[rows, :], xh[other, :], xl[other, :])
            return carry

        lax.fori_loop(0, 4, product, 0)
        result(acc).start()

    for q in range(4):
        @pl.when(schur & (c != q))
        def _(q=q):
            for s in range(2):
                arrived(topped(nn.at[s], q), R_NNY + 4 * s + q)

    @pl.when(lower)
    def _():
        result(acc).wait()

    for cond, wait in pending:
        pl.when(cond)(wait)


def fronts(picks, front, child):
    anywhere = pl.BlockSpec(memory_space=pl.ANY)
    return pl.pallas_call(
        front_kernel,
        out_shape=[jax.ShapeDtypeStruct((T, T), jnp.float32), jax.ShapeDtypeStruct((2, T, T), jnp.bfloat16)],
        in_specs=[pl.BlockSpec(memory_space=pltpu.SMEM)] + [anywhere] * 2,
        out_specs=[anywhere] * 2,
        scratch_shapes=[
            pltpu.VMEM((T, QR), jnp.float32),
            pltpu.VMEM((2, T, QR), jnp.bfloat16),
            pltpu.VMEM((3, T, QR), jnp.float32),
            pltpu.VMEM((2 * T, T), jnp.float32),
            pltpu.VMEM((STEPS, NB, T), jnp.float32),
            pltpu.VMEM((T, T), jnp.float32),
            pltpu.VMEM((2 * T, T), jnp.bfloat16),
            pltpu.VMEM((2 * T, T), jnp.bfloat16),
            pltpu.VMEM((NB, T), jnp.bfloat16),
            pltpu.VMEM((NB, T), jnp.bfloat16),
            pltpu.VMEM((NB, 2 * NB), jnp.float32),
            pltpu.VMEM((NB, NB), jnp.float32),
            pltpu.VMEM((NB, NB), jnp.float32),
            pltpu.SemaphoreType.DMA((N_SEND,)),
            pltpu.SemaphoreType.DMA((N_RECV,)),
            pltpu.SemaphoreType.DMA((4,)),
        ],
        compiler_params=pltpu.CompilerParams(
            collective_id=0, has_side_effects=True, vmem_limit_bytes=50 * 2**20
        ),
    )(picks, front, child)


def place_kernel(places, value, nn, out, kids, acc, sem, insem, osem):
    r, c = lax.axis_index("row"), lax.axis_index("col")
    schur = (r >= 1) & (c >= 1)
    parts = [pl.ds(i * QR, QR) for i in range(4)]
    get_kids = [
        pltpu.make_async_copy(nn.at[:, pl.ds(0, QR * (q + 1)), parts[q]], kids.at[:, pl.ds(0, QR * (q + 1)), parts[q]], sem.at[q])
        for q in range(4)
    ]
    get = [pltpu.make_async_copy(value.at[parts[i]], acc.at[parts[i]], insem.at[i]) for i in range(4)]
    put = [pltpu.make_async_copy(acc.at[parts[i]], out.at[parts[i]], osem.at[i]) for i in range(4)]

    @pl.when(schur)
    def _():
        for copy in get_kids:
            copy.start()

    for copy in get:
        copy.start()

    @pl.when(schur)
    def _():
        for copy in get_kids:
            copy.wait()

    for n in range(4):
        get[n].wait()

        @pl.when(schur)
        def _(n=n):
            def add_rows(b, carry):
                rows = pl.ds(pl.multiple_of(b * NB, NB), NB)
                for s in range(2):
                    j = places[s, STEPS * r + b]

                    @pl.when(j >= 0)
                    def _(s=s, j=j):
                        for d in range(STEPS):
                            i = places[s, STEPS * c + d]
                            above = lax.div(jnp.maximum(i, 0), 2) >= lax.div(j, 2)
                            at_j, at_i = (pl.ds(pl.multiple_of(x * NB, NB), NB) for x in (j, i))

                            @pl.when((i >= 0) & above)
                            def _(s=s, d=d):
                                acc[rows, pl.ds(d * NB, NB)] += kids[s, at_j, at_i].astype(jnp.float32)

                            @pl.when((i >= 0) & jnp.logical_not(above))
                            def _(s=s, d=d):
                                acc[rows, pl.ds(d * NB, NB)] += kids[s, at_i, at_j].astype(jnp.float32).T
                return carry

            lax.fori_loop(2 * n, 2 * n + 2, add_rows, 0)

        put[n].start()
    for copy in put:
        copy.wait()


def place(places, value, nn):
    anywhere = pl.BlockSpec(memory_space=pl.ANY)
    return pl.pallas_call(
        place_kernel,
        out_shape=jax.ShapeDtypeStruct((T, T), jnp.float32),
        in_specs=[pl.BlockSpec(memory_space=pltpu.SMEM)] + [anywhere] * 2,
        out_specs=anywhere,
        scratch_shapes=[
            pltpu.VMEM((2, T, T), jnp.bfloat16),
            pltpu.VMEM((T, T), jnp.float32),
            pltpu.SemaphoreType.DMA((4,)),
            pltpu.SemaphoreType.DMA((4,)),
            pltpu.SemaphoreType.DMA((4,)),
        ],
        compiler_params=pltpu.CompilerParams(vmem_limit_bytes=20 * 2**20),
    )(places, value, nn)


def local(front_entries, child_updates, child_maps):
    found = child_maps[:, :STEPS, None] == jnp.arange(4 * STEPS, dtype=jnp.int32)[None, None, :]
    order = jnp.arange(1, STEPS + 1, dtype=jnp.int32)
    places = jnp.sum(jnp.where(found, order[None, :, None], 0), axis=1) - 1
    picks = jnp.swapaxes(found, 1, 2).astype(jnp.float32).reshape(8 * STEPS, STEPS)
    return place(places, *fronts(picks, front_entries, child_updates))


def solution(mesh):
    placed = (P(("front", "row"), "col"), P(("front", "row"), "col"), P("front", None))
    return jax.shard_map(
        local, mesh=mesh, in_specs=placed, out_specs=P(("front", "row"), "col"), check_vma=False
    )
```

```python
import functools

import jax
import jax.numpy as jnp
from jax import lax
from jax.experimental import pallas as pl
from jax.experimental.pallas import tpu as pltpu
from jax.sharding import PartitionSpec as P

MESH = pl.DeviceIdType.MESH
HIGHEST = lax.Precision.HIGHEST
T = 1024
NB = 128
QR = 256
STEPS = T // NB
G = 8
HALF = T // 2

R_PIV = 0
R_FRONT = 16
R_NPA = 17
R_NNA = 18
R_NP = 19
R_NN = 21
R_ROWS = 23
R_CROSS = 27
R_PART = 33
R_NNY = 41
R_PAN = 49
R_PANY = 57
R_HALF = 89
R_HELP = 90
R_NPB = 92
R_NPC = 93
N_RECV = 94

S_PIV = 0
S_FRONT = 8
S_AHEAD = 12
S_NP = 16
S_NN = 19
S_RELAY = 21
S_ROWS = 22
S_CROSS = 25
S_PART = 29
S_NNY = 33
S_HALF = 39
S_ROOT = 40
S_PANZ = 80
S_PANY = 96
S_LAST = 120
S_PANM = 123
N_SEND = 131


def dot_t(a, b):
    return lax.dot_general(
        a, b, (((1,), (1,)), ((), ())), precision=HIGHEST, preferred_element_type=jnp.float32
    )


def split3(x):
    high = x.astype(jnp.bfloat16).astype(jnp.float32)
    rest = x - high
    middle = rest.astype(jnp.bfloat16).astype(jnp.float32)
    return high, middle, rest - middle


def eliminate_rows(g, work, upper, inverse):
    first = pl.multiple_of(g * G, G)
    rows = work[pl.ds(first, G), :]
    block, carried = rows[:, :NB], rows[:, NB:]
    turned = pltpu.roll(block, lax.rem(NB - first, NB), 1)
    sub = lax.broadcasted_iota(jnp.int32, (G, NB), 0)
    lane = lax.broadcasted_iota(jnp.int32, (G, NB), 1)
    columns = [jnp.broadcast_to(turned[:, j : j + 1], (G, NB)) for j in range(G)]
    scale = jnp.ones((G, NB), jnp.float32)
    for j in range(G):
        pivot = jnp.broadcast_to(columns[j][j : j + 1, :], (G, NB))
        scale = jnp.where(sub == j, pivot, scale)
        if j == G - 1:
            break
        factor = jnp.where(sub > j, columns[j] / pivot, 0.0)
        for i in range(j + 1, G):
            columns[i] = columns[i] - factor * columns[i][j : j + 1, :]
        block = block - factor * block[j : j + 1, :]
        carried = carried - factor * carried[j : j + 1, :]
    root = lax.rsqrt(scale)
    root = root * (1.5 - 0.5 * scale * root * root)
    block = jnp.where(lane >= first + sub, block * root, 0.0)
    carried = carried * root
    upper[pl.ds(first, G), :] = block
    inverse[pl.ds(first, G), :] = carried
    both = jnp.concatenate([block, carried], axis=1)
    high, middle, low = split3(both)
    left = jnp.concatenate(
        [high[:, :NB], high[:, :NB], middle[:, :NB], middle[:, :NB], high[:, :NB], low[:, :NB]], axis=0
    )
    right = jnp.concatenate([high, middle, high, middle, low, high], axis=0)
    work[...] -= jnp.dot(
        left.T.astype(jnp.bfloat16), right.astype(jnp.bfloat16), preferred_element_type=jnp.float32
    )


def split2(x):
    high = x.astype(jnp.bfloat16)
    return high, (x - high.astype(jnp.float32)).astype(jnp.bfloat16)


def dot3(ah, al, bh, bl):
    dims = (((1,), (1,)), ((), ()))
    one = lambda a, b: lax.dot_general(a, b, dims, preferred_element_type=jnp.float32)
    return one(ah, bh) + (one(ah, bl) + one(al, bh))


def front_kernel(
    picks, front, child, out, nn, fq, npq, bz, a, lp, acc, xh, xl, panh, panl, work, upper, inverse, ssem, rsem, lsem
):
    f, r, c = lax.axis_index("front"), lax.axis_index("row"), lax.axis_index("col")
    root = (r == 0) & (c == 0)
    lower = r >= 1
    odd = lax.rem(r, 2) == 1
    others = [1 + lax.rem(jnp.maximum(r, 1) - 1 + d, 3) for d in (1, 2)]
    around = [lax.rem(c + d, 4) for d in (1, 3, 2)]
    piv_source = odd & (c >= 2)
    child_source = (r == 0) | (r == 2)
    pending = []

    barrier = pltpu.get_barrier_semaphore()
    for row in range(4):
        for d in range(4):
            col = lax.rem(c + d, 4)

            @pl.when((row != r) | (d != 0))
            def _(row=row, col=col):
                pl.semaphore_signal(barrier, inc=1, device_id=(f, row, col), device_id_type=MESH)

    pl.semaphore_wait(barrier, 15)

    def remote(src, dst, sid, rid, row, col):
        return pltpu.make_async_remote_copy(
            src_ref=src, dst_ref=dst, send_sem=ssem.at[sid], recv_sem=rsem.at[rid],
            device_id=(f, row, col), device_id_type=MESH,
        )

    def send(cond, make, waited=True):
        @pl.when(cond)
        def _():
            make().start()

        pending.append((cond if waited is True else waited, lambda: make().wait_send()))

    def arrived(ref, rid):
        remote(ref, ref, 0, rid, lax.rem(r + 1, 4), c).wait_recv()

    def quarter(ref, q):
        return ref.at[:, pl.ds(pl.multiple_of(q * QR, QR), QR)]

    halves = [pl.ds(h * HALF, HALF) for h in range(2)]

    def topped(ref, q, at=None):
        return ref.at[pl.ds(0, QR * (q + 1)), pl.ds((q if at is None else at) * QR, QR)]

    sibling = lax.div(r, 2)
    own_front = lambda: pltpu.make_async_copy(quarter(front, 0), fq, lsem.at[0])
    own_tile = lambda: pltpu.make_async_copy(front, acc, lsem.at[2])
    own_child = lambda: pltpu.make_async_copy(quarter(child, 1), npq.at[sibling], lsem.at[1])
    own_np = child_source & (c == 2)
    own_nn = child_source & (c == 0)

    @pl.when(lower & (c == 0))
    def _():
        own_front().start()

    @pl.when(own_np)
    def _():
        own_child().start()

    @pl.when(root | (lower & (c >= 1)))
    def _():
        own_tile().start()

    for u in range(2):
        q_np = jnp.where(c < 2, 0, 7 - 2 * c - u)
        send(
            child_source & (c >= 2) & (q_np != c) & ((r != 0) | (q_np != 0)),
            lambda u=u, q=q_np: remote(quarter(child, u), npq.at[sibling], S_AHEAD + u, R_NPA, r, q),
        )

    for q in range(1, 4):
        send(
            child_source & (c == q // 2),
            lambda q=q: remote(topped(child, q, q % 2), topped(nn.at[sibling], q), S_AHEAD + q % 2, R_NNA, r, q),
        )

    send(
        (r == 0) & (c == 3),
        lambda: remote(quarter(child, 1).at[halves[0]], npq.at[1, halves[0]], S_AHEAD + 1, R_NPB, 0, 2),
    )
    for n, row in enumerate((1, 3, 2)):
        send(
            (r == 0) & (c == 3),
            lambda n=n, row=row: remote(quarter(child, 1).at[halves[1]], npq.at[0, halves[1]], S_LAST + n, R_NPC, row, 0),
        )

    for n, row in enumerate((1, 3)):
        send(root, lambda n=n, row=row: remote(topped(child, 0, 0), topped(nn.at[0], 0), S_NN + n, R_NN, row, 0))


    def cross(cond, src):
        for h, rows in enumerate(halves):
            for n, row in enumerate(others):
                send(
                    cond,
                    lambda h=h, n=n, row=row, rows=rows: remote(
                        src().at[rows], bz.at[r - 1, rows], S_CROSS + 2 * h + n, R_CROSS + 3 * h + r - 1, row, c
                    ),
                )

    first = lower & (c == 0)

    for h, col in enumerate((1, 3)):
        send(
            first,
            lambda h=h, col=col: remote(
                quarter(front, 2).at[halves[h]], bz.at[r - 1, halves[h]], S_FRONT + 2 * (col // 2), R_HELP + h, r, col
            ),
        )
    for n, q in enumerate((1, 3)):
        send(first, lambda n=n, q=q: remote(quarter(front, q), fq, S_FRONT + 1 + 2 * n, R_FRONT, r, q))

    for h, col in enumerate((1, 3)):
        @pl.when(lower & (c == col))
        def _(h=h):
            arrived(bz.at[r - 1, halves[h]], R_HELP + h)

        send(
            lower & (c == col),
            lambda h=h: remote(bz.at[r - 1, halves[h]], fq.at[halves[h]], S_RELAY, R_FRONT if h == 0 else R_HELP, r, 2),
        )

    def pivot_part(k):
        rows, t = pl.ds(0, T - k * NB), (STEPS - 1 - k) % 4
        return remote(
            child.at[rows, pl.ds(t * NB, NB)],
            xh.at[pl.ds(pl.multiple_of(sibling * T, T), T - k * NB), pl.ds((STEPS - 1 - k) * NB, NB)],
            S_PIV + k, R_PIV + sibling * 8 + k, 0, 0,
        )

    def pivot_parts(*panels):
        for k in panels:
            send(odd & (c == 3 - k // 4), lambda k=k: pivot_part(k))

    @pl.when(odd & (c == 3))
    def _():
        pivot_part(0).start()
        pivot_part(0).wait_send()

    pivot_parts(1)

    @pl.when(own_np)
    def _():
        own_child().wait()

    first_c = (r == 0) & (c != 0)

    @pl.when((first_c | (r == 2)) & (c != 2))
    def _():
        arrived(npq.at[sibling], R_NPA)

    for n, row in enumerate((1, 3, 2)):
        send(
            first_c if row == 2 else first_c | (r == 2),
            lambda n=n, row=row: remote(npq.at[sibling], npq.at[sibling], S_NP + n, R_NP + sibling, row, c),
        )

    @pl.when((r == 0) & (c == 2))
    def _():
        arrived(npq.at[1, halves[0]], R_NPB)

    for n, row in enumerate((1, 3, 2)):
        send(
            (r == 0) & (c == 2),
            lambda n=n, row=row: remote(npq.at[1, halves[0]], npq.at[0, halves[0]], S_LAST + n, R_NP, row, 0),
        )

    def other_columns(rows):
        for q in range(4):
            if q:
                @pl.when(rows & (c == q))
                def _(q=q):
                    arrived(topped(nn.at[sibling], q), R_NNA)

            for n, row in enumerate((1, 3)):
                src = (lambda q=q: topped(nn.at[sibling], q)) if q else (lambda: topped(child, 0, 0))
                send(
                    rows & (c == q),
                    lambda n=n, row=row, q=q, src=src: remote(
                        src(), topped(nn.at[sibling], q), S_NN + n, R_NN + sibling, row, c
                    ),
                )

    pivot_parts(2, 3)

    @pl.when(lower & ((c == 1) | (c == 3)))
    def _():
        arrived(fq, R_FRONT)

    @pl.when(lower & (c == 2))
    def _():
        arrived(fq.at[halves[0]], R_FRONT)
        arrived(fq.at[halves[1]], R_HELP)

    @pl.when(lower & (c != 0))
    def _():
        arrived(npq.at[0], R_NP)

    @pl.when(first)
    def _():
        arrived(npq.at[0, halves[0]], R_NP)
        arrived(npq.at[0, halves[1]], R_NPC)

    @pl.when(odd)
    def _():
        arrived(npq.at[1], R_NP + 1)

    cross(first, lambda: quarter(front, 0))
    cross(lower & (c != 0), lambda: fq)
    pivot_parts(4, 5, 6, 7)

    def assemble(source, target, row, low, high):
        def block(b, carry):
            rows = pl.ds(pl.multiple_of(b * NB, NB), NB)
            for t in range(2):
                value = source[rows, pl.ds(t * NB, NB)]
                for s in range(2):
                    for j in range(STEPS):
                        picked = picks[4 * STEPS * s + STEPS * row + b, j]
                        value += picked * npq[s, pl.ds(j * NB, NB), pl.ds((1 - t) * NB, NB)].astype(jnp.float32)
                target[rows, pl.ds(t * NB, NB)] = value
            return carry

        lax.fori_loop(low, high, block, 0)

    def rows_part(q):
        return quarter(a.at[pl.ds(0, T)], q)

    def cols_part(q):
        return quarter(a.at[pl.ds(T, T)], q)

    @pl.when(first)
    def _():
        own_front().wait()

    @pl.when(lower)
    def _():
        assemble(fq, rows_part(c), r, 0, STEPS)

    share_rows = lambda n: remote(rows_part(c), rows_part(c), S_ROWS + n, R_ROWS + c, r, around[n])

    @pl.when(lower)
    def _():
        for n in range(3):
            share_rows(n).start()

    def share(ref, k, q):
        return ref.at[k, pl.ds(q * 32, 32), pl.ds(0, NB * (k + 1))]

    def pass_on(k):
        @pl.when(jnp.logical_not(root))
        def _():
            arrived(share(lp, k, c), R_PAN + k)

        for n, row in enumerate((1, 3)):
            send(
                first_c,
                lambda k=k, n=n, row=row: remote(share(lp, k, c), share(lp, k, c), S_PANZ + 2 * k + n, R_PAN + k, row, c),
            )
        send(first_c, lambda: remote(share(lp, k, c), share(lp, k, c), S_PANM + k, R_PAN + k, 2, c))
        for n, col in enumerate(around):
            send(
                lower,
                lambda k=k, n=n, col=col: remote(
                    share(lp, k, c), share(lp, k, c), S_PANY + 3 * k + n, R_PANY + 4 * k + c, r, col
                ),
            )

    pass_on(0)
    pass_on(1)
    other_columns(first_c | (r == 2))

    for h, half in enumerate(halves):
        for n, row in enumerate(others):
            @pl.when(lower)
            def _(h=h, half=half, row=row):
                arrived(bz.at[row - 1, half], R_CROSS + 3 * h + row - 1)

            @pl.when(lower & (c != row))
            def _(h=h, row=row):
                assemble(bz.at[row - 1], bz.at[row - 1], row, 4 * h, 4 * h + 4)

            @pl.when(lower & (c == row))
            def _(h=h, row=row):
                assemble(bz.at[row - 1], cols_part(c), row, 4 * h, 4 * h + 4)

            send(
                lower & (c != row),
                lambda h=h, half=half, n=n, row=row: remote(
                    bz.at[row - 1, half], cols_part(c).at[half], S_PART + 2 * h + n, R_PART + 4 * h + c, r, row
                ),
            )
        if h == 0:
            pass_on(2)
            pass_on(3)

    def to_row(s, cond, q, src):
        for n, col in enumerate(around):
            send(
                cond & (c == q) & (col != 0),
                lambda n=n, col=col: remote(
                    src(), topped(nn.at[s], q), S_NNY + 3 * s + n, R_NNY + 4 * s + c, r, col
                ),
            )

    for q in range(4):
        size = QR * (q + 1) // 2
        columns = pl.ds(q * QR, QR)
        ends = [(pl.ds(0, size), columns), (pl.ds(size, size), columns)]
        to_row(1, r == 2, q, (lambda q=q: topped(nn.at[1], q)) if q else (lambda: topped(child, 0, 0)))

        @pl.when(odd & (c == q))
        def _(q=q):
            arrived(topped(nn.at[1], q), R_NN + 1)

        to_row(1, odd, q, lambda q=q: topped(nn.at[1], q))

        @pl.when(odd & (c == q))
        def _(q=q):
            arrived(topped(nn.at[0], q), R_NN)

        for row, end, rid in ((1, 0, R_NN), (3, 1, R_HALF)):
            send(
                (r == row) & (c == q),
                lambda end=end, rid=rid, ends=ends: remote(nn.at[(0,) + ends[end]], nn.at[(0,) + ends[end]], S_HALF, rid, 2, c),
            )

        @pl.when((r == 2) & (c == q))
        def _(ends=ends):
            arrived(nn.at[(0,) + ends[0]], R_NN)
            arrived(nn.at[(0,) + ends[1]], R_HALF)

        to_row(0, lower, q, lambda q=q: topped(nn.at[0], q))
    lone = (c == 0) | (c == r)
    away = lower & jnp.logical_not(lone)

    def solve(k, base):
        done, here, all_here = pl.ds(0, k * NB), pl.ds(k * NB, NB), pl.ds(0, NB * (k + 1))
        panh[:, all_here], panl[:, all_here] = split2(lp[k, :, all_here])

        def chunk(i, carry):
            rows = pl.ds(pl.multiple_of(base + i * QR, QR), QR)
            value = a[rows, here]
            if k:
                value = value - dot3(xh[rows, done], xl[rows, done], panh[:, done], panl[:, done])
            vh, vl = split2(value)
            solved = dot3(vh, vl, panh[:, here], panl[:, here])
            a[rows, here] = solved
            xh[rows, here], xl[rows, here] = split2(solved)
            return carry

        lax.fori_loop(0, T // QR, chunk, 0)

    @pl.when(lower)
    def _():
        for n in range(3):
            share_rows(n).wait_send()
        for q in around:
            arrived(rows_part(q), R_ROWS + q)

    def solve_rows(*steps):
        @pl.when(lower)
        def _():
            for k in steps:
                for q in around:
                    arrived(share(lp, k, q), R_PANY + 4 * k + q)
                solve(k, 0)

    pass_on(4)
    pass_on(5)
    pass_on(6)
    pass_on(7)
    solve_rows(0, 1, 2, 3, 4, 5, 6)

    @pl.when(away)
    def _():
        for h, half in enumerate(halves):
            for q in around:
                arrived(cols_part(q).at[half], R_PART + 4 * h + q)
        for k in range(STEPS - 1):
            solve(k, T)

    schur = lower & (c >= 1)

    def schur_product(start, stop):
        second, over = jnp.where(lone, 0, T), pl.ds(start, stop - start)

        def product(i, carry):
            rows = pl.ds(pl.multiple_of(i * QR, QR), QR)
            for j in range(4):
                other = pl.ds(pl.multiple_of(second + j * QR, QR), QR)
                columns = pl.ds(j * QR, QR)
                acc[rows, columns] -= dot3(xh[rows, over], xl[rows, over], xh[other, over], xl[other, over])
            return carry

        lax.fori_loop(0, 4, product, 0)

    @pl.when(schur)
    def _():
        own_tile().wait()
        schur_product(0, T - NB)

    solve_rows(7)

    @pl.when(away)
    def _():
        solve(STEPS - 1, T)


    def root_sends(k):
        made = []
        for q in (1, 3, 2):
            made.append(remote(share(lp, k, q), share(lp, k, q), S_ROOT + 5 * k + q - 1, R_PAN + k, 0, q))
        for sid, row in ((S_ROOT + 5 * k + 3, 1), (S_ROOT + 5 * k + 4, 3), (S_PANM + k, 2)):
            made.append(remote(share(lp, k, 0), share(lp, k, 0), sid, R_PAN + k, row, 0))
        return made

    result = lambda ref: pltpu.make_async_copy(ref, out, lsem.at[3])

    @pl.when(root)
    def _():
        low = a.at[pl.ds(0, T)]
        low[...] = jnp.zeros((T, T), jnp.float32)
        own_tile().wait()
        ones = (
            lax.broadcasted_iota(jnp.int32, (NB, NB), 0) == lax.broadcasted_iota(jnp.int32, (NB, NB), 1)
        ).astype(jnp.float32)
        for k in range(STEPS):
            done, here, there = pl.ds(0, k * NB), pl.ds(k * NB, NB), pl.ds((STEPS - 1 - k) * NB, NB)
            for s in range(2):
                arrived(xh.at[pl.ds(s * T, T - k * NB), there], R_PIV + s * 8 + k)

            def updated(i, k=k, done=done, here=here, there=there):
                rows = pl.ds(pl.multiple_of(i * NB, NB), NB)
                value = acc[rows, here]
                for s in range(2):
                    source = pl.ds(pl.multiple_of(s * T + (STEPS - 1 - i) * NB, NB), NB)
                    value = value + xh[source, there].astype(jnp.float32)
                if k:
                    value = value - dot_t(low[rows, done], low[here, done])
                return value

            work[:, :NB] = updated(k)
            work[:, NB:] = ones

            def group(g, carry):
                eliminate_rows(g, work, upper, inverse)
                return carry

            lax.fori_loop(0, NB // G, group, 0)
            low[here, here] = upper[...].T
            if k:
                lp[k, :, done] = low[here, done]
            lp[k, :, here] = inverse[...]
            for copy in root_sends(k):
                copy.start()

            def below(i, carry, updated=updated, here=here):
                low[pl.ds(pl.multiple_of(i * NB, NB), NB), here] = dot_t(updated(i), inverse[...])
                return carry

            if k + 1 < STEPS:
                lax.fori_loop(k + 1, STEPS, below, 0)
        result(low).start()
        result(low).wait()
        for k in range(STEPS):
            for copy in root_sends(k):
                copy.wait_send()

    @pl.when(first_c)
    def _():
        acc[...] = jnp.zeros_like(acc)
        result(acc).start()
        result(acc).wait()

    @pl.when(first)
    def _():
        result(a.at[pl.ds(0, T)]).start()

    @pl.when(schur)
    def _():
        schur_product(T - NB, T)
        result(acc).start()

    for q in range(4):
        @pl.when(schur & (c != q))
        def _(q=q):
            for s in range(2):
                arrived(topped(nn.at[s], q), R_NNY + 4 * s + q)

    @pl.when(lower)
    def _():
        result(acc).wait()

    for cond, wait in pending:
        pl.when(cond)(wait)


def fronts(picks, front, child):
    anywhere = pl.BlockSpec(memory_space=pl.ANY)
    return pl.pallas_call(
        front_kernel,
        out_shape=[jax.ShapeDtypeStruct((T, T), jnp.float32), jax.ShapeDtypeStruct((2, T, T), jnp.bfloat16)],
        in_specs=[pl.BlockSpec(memory_space=pltpu.SMEM)] + [anywhere] * 2,
        out_specs=[anywhere] * 2,
        scratch_shapes=[
            pltpu.VMEM((T, QR), jnp.float32),
            pltpu.VMEM((2, T, QR), jnp.bfloat16),
            pltpu.VMEM((3, T, QR), jnp.float32),
            pltpu.VMEM((2 * T, T), jnp.float32),
            pltpu.VMEM((STEPS, NB, T), jnp.float32),
            pltpu.VMEM((T, T), jnp.float32),
            pltpu.VMEM((2 * T, T), jnp.bfloat16),
            pltpu.VMEM((2 * T, T), jnp.bfloat16),
            pltpu.VMEM((NB, T), jnp.bfloat16),
            pltpu.VMEM((NB, T), jnp.bfloat16),
            pltpu.VMEM((NB, 2 * NB), jnp.float32),
            pltpu.VMEM((NB, NB), jnp.float32),
            pltpu.VMEM((NB, NB), jnp.float32),
            pltpu.SemaphoreType.DMA((N_SEND,)),
            pltpu.SemaphoreType.DMA((N_RECV,)),
            pltpu.SemaphoreType.DMA((4,)),
        ],
        compiler_params=pltpu.CompilerParams(
            collective_id=0, has_side_effects=True, vmem_limit_bytes=50 * 2**20
        ),
    )(picks, front, child)


def place_kernel(places, value, nn, out, kids, acc, sem, insem, osem):
    r, c = lax.axis_index("row"), lax.axis_index("col")
    schur = (r >= 1) & (c >= 1)
    parts = [pl.ds(i * QR, QR) for i in range(4)]
    get_kids = [
        pltpu.make_async_copy(nn.at[:, pl.ds(0, QR * (q + 1)), parts[q]], kids.at[:, pl.ds(0, QR * (q + 1)), parts[q]], sem.at[q])
        for q in range(4)
    ]
    get = [pltpu.make_async_copy(value.at[parts[i]], acc.at[parts[i]], insem.at[i]) for i in range(4)]
    put = [pltpu.make_async_copy(acc.at[parts[i]], out.at[parts[i]], osem.at[i]) for i in range(4)]

    @pl.when(schur)
    def _():
        for copy in get_kids:
            copy.start()

    for copy in get:
        copy.start()

    @pl.when(schur)
    def _():
        for copy in get_kids:
            copy.wait()

    for n in range(4):
        get[n].wait()

        @pl.when(schur)
        def _(n=n):
            def add_rows(b, carry):
                rows = pl.ds(pl.multiple_of(b * NB, NB), NB)
                for s in range(2):
                    j = places[s, STEPS * r + b]

                    @pl.when(j >= 0)
                    def _(s=s, j=j):
                        for d in range(STEPS):
                            i = places[s, STEPS * c + d]
                            above = lax.div(jnp.maximum(i, 0), 2) >= lax.div(j, 2)
                            at_j, at_i = (pl.ds(pl.multiple_of(x * NB, NB), NB) for x in (j, i))

                            @pl.when((i >= 0) & above)
                            def _(s=s, d=d):
                                acc[rows, pl.ds(d * NB, NB)] += kids[s, at_j, at_i].astype(jnp.float32)

                            @pl.when((i >= 0) & jnp.logical_not(above))
                            def _(s=s, d=d):
                                acc[rows, pl.ds(d * NB, NB)] += kids[s, at_i, at_j].astype(jnp.float32).T
                return carry

            lax.fori_loop(2 * n, 2 * n + 2, add_rows, 0)

        put[n].start()
    for copy in put:
        copy.wait()


def place(places, value, nn):
    anywhere = pl.BlockSpec(memory_space=pl.ANY)
    return pl.pallas_call(
        place_kernel,
        out_shape=jax.ShapeDtypeStruct((T, T), jnp.float32),
        in_specs=[pl.BlockSpec(memory_space=pltpu.SMEM)] + [anywhere] * 2,
        out_specs=anywhere,
        scratch_shapes=[
            pltpu.VMEM((2, T, T), jnp.bfloat16),
            pltpu.VMEM((T, T), jnp.float32),
            pltpu.SemaphoreType.DMA((4,)),
            pltpu.SemaphoreType.DMA((4,)),
            pltpu.SemaphoreType.DMA((4,)),
        ],
        compiler_params=pltpu.CompilerParams(vmem_limit_bytes=20 * 2**20),
    )(places, value, nn)


def local(front_entries, child_updates, child_maps):
    found = child_maps[:, :STEPS, None] == jnp.arange(4 * STEPS, dtype=jnp.int32)[None, None, :]
    order = jnp.arange(1, STEPS + 1, dtype=jnp.int32)
    places = jnp.sum(jnp.where(found, order[None, :, None], 0), axis=1) - 1
    picks = jnp.swapaxes(found, 1, 2).astype(jnp.float32).reshape(8 * STEPS, STEPS)
    return place(places, *fronts(picks, front_entries, child_updates))


def solution(mesh):
    placed = (P(("front", "row"), "col"), P(("front", "row"), "col"), P("front", None))
    return jax.shard_map(
        local, mesh=mesh, in_specs=placed, out_specs=P(("front", "row"), "col"), check_vma=False
    )
```
